512 devices in a mesh: blk: 64 (over x_hi, z, core), help: 8 (over y, x_lo).
Axes of the slice: x: 4 (x_hi: 2, x_lo: 2; x = x_hi * 2 + x_lo), y: 4, z: 16, core: 2. Of those that a mesh axis runs over, the one named last changes fastest.
Arguments:
- features_t: bfloat16 [256, 98304], P(None, 'blk'), may hold values from -6 to 6
- weight: bfloat16 [256, 256], replicated, may hold values from -0.375 to 0.375
- bias: float32 [256], P('help'), may hold values from -3 to 3
- cotangent_t: bfloat16 [256, 98304], P('help', 'blk'), may hold values from -6 to 6
- tile_vals: bfloat16 [64, 8, 80, 128, 128], P('blk', 'help'), may hold values from -0.078125 to 0.078125
- slot_row: int32 [64, 8, 80], P('blk', 'help'), may hold values from 0 to 12, as said below
- slot_col: int32 [64, 8, 80], P('blk', 'help'), may hold values from 0 to 59, as said below
Outputs:
- output_t: bfloat16 [256, 98304], P('help', 'blk')
- propagated_grad: float32 [256, 98304], P('help', 'blk')
- weight_grad: float32 [256, 256], P(None, 'help')
- bias_grad: float32 [256], P('help')
The draws below stay inside these ranges and needn't reach their ends.
Inputs may be any that keep to these rules, and one draw needn't show every extreme that they name: `slot_row`: each device has 80 slots, the used ones first; a slot holding 12 is unused. In every node-row block one helper uses all 80 slots and every other one at least 40. A slot's column tile is tile slot_col % 12 of node-row block (own block + slot_col // 12 - 2) taken around the loop of 64 blocks.
All inputs are finite; a program needn't handle non-finite values.
Results may differ from the reference program's by a relative error of at most 0.0045.
Values may be sent and summed in bfloat16 or wider, within the bound.
No kernel may reach another device: no remote copies, remote signals or barrier semaphores. Data moves between devices by JAX's collectives and lax.ppermute only.
A program may use at most 64 MiB of HBM per device.

```python
import math
import jax
import jax.numpy as jnp
from jax import lax

F = 256
TILE = 128
BAND = 2
TR = 12
KD = 80
GROUPS = 64
HELPERS = 8
NODES = 98304
N_BLK = 64


def slot_plan(key):
    base = jax.random.fold_in(key, 11)
    key_perm, key_pick, key_count, key_full, key_col = jax.random.split(base, 5)
    perms = jax.vmap(lambda sub: jax.random.permutation(sub, TR))(jax.random.split(key_perm, GROUPS))
    picks = jax.random.randint(key_pick, (2, GROUPS, HELPERS, KD), 0, TR)
    ranks = jnp.minimum(picks[0], picks[1])
    spread_perms = jnp.broadcast_to(perms[:, None, :], (GROUPS, HELPERS, TR))
    rows = jnp.take_along_axis(spread_perms, ranks, axis=2)
    counts = jax.random.randint(key_count, (GROUPS, HELPERS), KD // 2, KD + 1)
    fullest = jax.random.randint(key_full, (GROUPS, 1), 0, HELPERS)
    counts = jnp.where(jnp.arange(HELPERS, dtype=jnp.int32)[None, :] == fullest, KD, counts)
    used = jnp.arange(KD, dtype=jnp.int32)[None, None, :] < counts[:, :, None]
    rows = jnp.where(used, rows, TR).astype(jnp.int32)
    cols = jax.random.randint(key_col, (GROUPS, HELPERS, KD), 0, (2 * BAND + 1) * TR).astype(jnp.int32)
    return (rows, cols)


def draw_slot_row(key, part):
    return slot_plan(key)[0]


def draw_slot_col(key, part):
    return slot_plan(key)[1]


def levels(own_key, extent, cuts, low, high):
    def one(position, blocks):
        steps = jax.random.uniform(jax.random.fold_in(jax.random.fold_in(own_key, 6), position), (blocks,), jnp.float32, low / len(cuts), high / len(cuts))
        return jnp.repeat(jnp.exp(steps), extent[position] // blocks).reshape((-1,) + (1,) * (len(extent) - position - 1))

    gain = one(*cuts[0])
    for cut in cuts[1:]:
        gain = gain * one(*cut)
    return gain


def centred(key, dims, scale, bound, cuts=(), kind=jnp.bfloat16):
    entries = jax.random.normal(key, dims, jnp.float32) * scale
    if len(cuts) > 0:
        entries = levels(key, dims, cuts, -0.22, 0.18) * entries
    return jnp.clip(entries, min=-bound, max=bound).astype(kind)


def setup_inputs(seed: int = 0) -> dict:
    key_of = jax.random.split(jax.random.key(seed), 8)
    features_t = centred(key_of[0], (F, NODES), 1.0, 6.0, ((1, 64),))
    weight = centred(key_of[1], (F, F), F ** -0.5, 0.375)
    bias = centred(key_of[2], (F,), 0.5, 3.0, ((0, 8),), jnp.float32)
    cotangent_t = centred(key_of[3], (F, NODES), 1.0, 6.0, ((0, 8), (1, 64)))
    tile_vals = centred(key_of[4], (GROUPS, HELPERS, KD, TILE, TILE), (TILE * KD * HELPERS // TR) ** -0.5, 0.078125, ((0, 64), (1, 8)))
    slot_row = draw_slot_row(jax.random.fold_in(key_of[7], 71), 0)
    slot_col = draw_slot_col(jax.random.fold_in(key_of[7], 71), 0)
    return dict(features_t=features_t, weight=weight, bias=bias, cotangent_t=cotangent_t, tile_vals=tile_vals, slot_row=slot_row, slot_col=slot_col)


def propagate(source_t, tile_vals, slot_row, slot_col):
    width = source_t.shape[0]
    tile = tile_vals.shape[-1]
    rows_block = TR * tile
    blocks = source_t.reshape(width, N_BLK, rows_block)
    offsets = jnp.arange(-BAND, BAND + 1, dtype=jnp.int32)

    def one_group(items):
        index, group_tiles, group_rows, group_cols = items
        chosen = ((index + offsets) % N_BLK).astype(jnp.int32)
        window = jnp.take(blocks, chosen, axis=1).reshape(width, (2 * BAND + 1) * rows_block)
        tiles = group_tiles.reshape(-1, tile, tile)
        rows = group_rows.reshape(-1)
        cols = group_cols.reshape(-1)
        pieces = jax.vmap(lambda column: lax.dynamic_slice_in_dim(window, column * tile, tile, 1))(cols)
        products = jnp.einsum('kfc,krc->kfr', pieces.astype(jnp.float32), tiles.astype(jnp.float32), precision=lax.Precision.HIGHEST)
        onehot = (rows[None, :] == jnp.arange(TR, dtype=jnp.int32)[:, None]).astype(jnp.float32)
        summed = jnp.einsum('tk,kfr->ftr', onehot, products, precision=lax.Precision.HIGHEST)
        return summed.reshape(width, rows_block)
    indices = jnp.arange(N_BLK, dtype=jnp.int32)
    per_group = lax.map(one_group, (indices, tile_vals, slot_row, slot_col))
    return jnp.transpose(per_group, (1, 0, 2)).reshape(width, N_BLK * rows_block)

def reference(features_t, weight, bias, cotangent_t, tile_vals, slot_row, slot_col):
    agg_t = propagate(features_t, tile_vals, slot_row, slot_col).astype(jnp.bfloat16)
    pre = jnp.dot(weight.T, agg_t, preferred_element_type=jnp.float32) + bias.astype(jnp.float32)[:, None]
    output_t = jax.nn.elu(pre).astype(jnp.bfloat16)
    slope = jnp.where(pre > 0.0, jnp.ones_like(pre), jnp.exp(jnp.minimum(pre, 0.0)))
    grad_pre = (cotangent_t.astype(jnp.float32) * slope).astype(jnp.bfloat16)
    scale = 1.0 / math.sqrt(NODES)
    weight_grad = jnp.dot(agg_t, grad_pre.T, preferred_element_type=jnp.float32) * scale
    bias_grad = lax.optimization_barrier(jnp.sum(grad_pre.astype(jnp.float32), axis=1)) * scale
    back = jnp.dot(weight, grad_pre, preferred_element_type=jnp.float32).astype(jnp.bfloat16)
    propagated_grad = propagate(back, tile_vals, slot_row, slot_col)
    return (output_t, propagated_grad, weight_grad, bias_grad)
```

```python
import functools
import math

import jax
import jax.numpy as jnp
from jax import lax
from jax.experimental import pallas as pl
from jax.experimental.pallas import tpu as pltpu
from jax.sharding import PartitionSpec as P

BAND = 2
AXES = ("blk", "help")
ANY = pl.BlockSpec(memory_space=pl.ANY)
VMEM = pl.BlockSpec(memory_space=pltpu.VMEM)
SMEM = pl.BlockSpec(memory_space=pltpu.SMEM)
NT = (((1,), (1,)), ((), ()))
NN = (((1,), (0,)), ((), ()))
TN = (((0,), (0,)), ((), ()))
UNROLL = 8


def move(block, source):
    blks, helps = lax.axis_size("blk"), lax.axis_size("help")
    route = []
    for b in range(blks):
        for h in range(helps):
            sb, sh = source(b, h)
            route.append(((sb % blks) * helps + sh, b * helps + h))
    return lax.ppermute(block, AXES, route)


def step_two(b, h, sign, blks):
    other = (b + 2 * sign) % blks
    half = blks // 2
    return (other, h if other // half == b // half else h ^ 1)


def window(block):
    blks = lax.axis_size("blk")
    swap = lambda b, h: (b ^ 1, h)
    one = move(block, lambda b, h: step_two(b, h, 1 if b % 2 == 0 else -1, blks))
    zero = move(block, swap)
    two = move(block, lambda b, h: step_two(b, h, -1 if b % 2 == 0 else 1, blks))
    three = move(one, swap)
    return (block, zero, one, two, three)


def load_all(refs, win, tiles, tiles_v, sems):
    copies = [pltpu.make_async_copy(ref, win.at[i], sems.at[i]) for i, ref in enumerate(refs)]
    copies.append(pltpu.make_async_copy(tiles, tiles_v, sems.at[len(refs)]))
    for copy in copies:
        copy.start()
    return copies


def add_slots(rows, bufs, cols, tiles_v, acc, piece, dims):
    slots, tile = tiles_v.shape[0], tiles_v.shape[1]

    @pl.loop(0, slots // UNROLL)
    def _(step):
        for j in range(UNROLL):
            k = step * UNROLL + j
            product = lax.dot_general(
                tiles_v[k],
                piece(bufs[k], pl.multiple_of(cols[k] * tile, tile)),
                dims,
                preferred_element_type=jnp.float32,
            )
            place = pl.ds(pl.multiple_of(rows[k] * tile, tile), tile)
            acc[place, :] += product


def forward_kernel(rows, bufs, cols, b0, b1, b2, b3, b4, tiles, out, win, tiles_v, acc, sems):
    tile = tiles_v.shape[1]
    copies = load_all((b0, b1, b2, b3, b4), win, tiles, tiles_v, sems)
    acc[...] = jnp.zeros_like(acc)
    for copy in copies:
        copy.wait()
    add_slots(rows, bufs, cols, tiles_v, acc, lambda s, c: win[s, :, pl.ds(c, tile)], NT)
    out[...] = acc[: out.shape[0], :].astype(jnp.bfloat16)


def backward_kernel(rows, bufs, cols, b0, b1, b2, b3, b4, tiles, out, win, tiles_v, acc, sems):
    tile = tiles_v.shape[1]
    copies = load_all((b0, b1, b2, b3, b4), win, tiles, tiles_v, sems)
    acc[...] = jnp.zeros_like(acc)
    for copy in copies:
        copy.wait()
    add_slots(rows, bufs, cols, tiles_v, acc, lambda s, c: win[s, pl.ds(c, tile), :], NN)
    width = out.shape[0]
    eye = (
        lax.broadcasted_iota(jnp.int32, (width, width), 0)
        == lax.broadcasted_iota(jnp.int32, (width, width), 1)
    ).astype(jnp.bfloat16)
    for t in range(out.shape[1] // tile):
        part = acc[t * tile : (t + 1) * tile, :].astype(jnp.bfloat16)
        out[:, t * tile : (t + 1) * tile] = lax.dot_general(
            eye, part, NT, preferred_element_type=jnp.float32
        ).astype(jnp.bfloat16)


def aggregate(kernel, blocks, tiles, slots, out_shape):
    count, tile = tiles.shape[0], tiles.shape[1]
    nodes = max(blocks[0].shape)
    width = min(blocks[0].shape)
    return pl.pallas_call(
        kernel,
        out_shape=jax.ShapeDtypeStruct(out_shape, jnp.bfloat16),
        in_specs=[SMEM] * 3 + [ANY] * 6,
        out_specs=VMEM,
        scratch_shapes=[
            pltpu.VMEM((5,) + blocks[0].shape, jnp.bfloat16),
            pltpu.VMEM(tiles.shape, jnp.bfloat16),
            pltpu.VMEM((nodes + tile, width), jnp.float32),
            pltpu.SemaphoreType.DMA((6,)),
        ],
        compiler_params=pltpu.CompilerParams(vmem_limit_bytes=24 * 2**20),
        cost_estimate=pl.CostEstimate(
            flops=2 * count * tile * tile * width,
            bytes_accessed=10 * 2**20,
            transcendentals=0,
        ),
    )(*slots, *blocks, tiles)


def middle_kernel(parts, cotb, weight, weight_t, out, back, grads):
    nodes = parts.shape[1]
    total = parts[0].astype(jnp.float32)
    for s in range(1, parts.shape[0]):
        total = total + parts[s].astype(jnp.float32)
    agg = total.astype(jnp.bfloat16)
    extra = cotb[:, nodes:].astype(jnp.float32)
    bias = extra[:, 0:1] + extra[:, 1:2] + extra[:, 2:3]
    pre = lax.dot_general(weight_t[...], agg, NT, preferred_element_type=jnp.float32) + bias
    decay = jnp.exp(jnp.minimum(pre, 0.0))
    out[...] = jnp.where(pre > 0.0, pre, decay - 1.0).astype(jnp.bfloat16)
    slope = jnp.where(pre > 0.0, 1.0, decay)
    grad = (cotb[:, :nodes].astype(jnp.float32) * slope).astype(jnp.bfloat16)
    back_n = lax.dot_general(
        grad, weight_t[...], TN, preferred_element_type=jnp.float32
    ).astype(jnp.bfloat16)
    for s in range(back.shape[0]):
        back[s] = back_n
    width = agg.shape[1]
    grads[:, :width] = lax.dot_general(grad, agg, NN, preferred_element_type=jnp.float32)
    ones = jnp.ones((nodes, grads.shape[1] - width), jnp.bfloat16)
    grads[:, width:] = lax.dot_general(grad, ones, NN, preferred_element_type=jnp.float32)


def spread(x):
    return lax.all_to_all(x, "help", 0, 0)


def per_device(features_t, weight, bias, cotangent_t, tile_vals, slot_row, slot_col):
    tiles = tile_vals[0, 0]
    tile = tiles.shape[-1]
    width, nodes = features_t.shape
    row_tiles = nodes // tile
    helps = lax.axis_size("help")
    blks = lax.axis_size("blk")
    share = cotangent_t.shape[0]
    mine = nodes // helps

    odd = lax.axis_index("blk") % 2
    span = slot_col[0, 0] // row_tiles
    place = jnp.where(
        odd == 0,
        jnp.array([3, 4, 0, 1, 2], jnp.int32)[span],
        jnp.array([2, 1, 0, 4, 3], jnp.int32)[span],
    )
    slots = (slot_row[0, 0], place, slot_col[0, 0] % row_tiles)

    high = lax.reduce_precision(bias, 8, 7)
    middle = lax.reduce_precision(bias - high, 8, 7)
    low = bias - high - middle
    parts = jnp.stack([high, middle, low], axis=1).astype(jnp.bfloat16)
    lanes = 2 * tile
    cot = cotangent_t.reshape(share, helps, mine).transpose(1, 0, 2)
    tail = jnp.broadcast_to(
        jnp.pad(parts, ((0, 0), (0, lanes - mine - 3)))[None], (helps, share, lanes - mine)
    )
    cotb = spread(jnp.concatenate([cot, tail], axis=2)).reshape(width, lanes)

    partial_value = aggregate(
        forward_kernel, window(features_t), tiles, slots, (nodes, width)
    )
    received = spread(partial_value.reshape(helps, mine, width))
    out, back, grads = pl.pallas_call(
        middle_kernel,
        out_shape=(
            jax.ShapeDtypeStruct((width, mine), jnp.bfloat16),
            jax.ShapeDtypeStruct((helps, mine, width), jnp.bfloat16),
            jax.ShapeDtypeStruct((width, width + tile), jnp.float32),
        ),
        in_specs=[VMEM] * 4,
        out_specs=(VMEM,) * 3,
    )(received, cotb, weight, weight.T)
    back_full = spread(back).reshape(nodes, width)
    back_partial = aggregate(
        backward_kernel, window(back_full), tiles, slots, (width, nodes)
    )
    summed = spread(back_partial.reshape(helps, share, nodes))
    propagated = jnp.sum(summed.astype(jnp.float32), axis=0)

    output = spread(out.reshape(helps, share, mine)).transpose(1, 0, 2).reshape(share, nodes)

    total = jnp.sum(spread(grads.reshape(helps, share, width + tile)), axis=0)
    step = 1
    while step < blks:
        total = total + move(total, functools.partial(lambda s, b, h: (b ^ s, h), step))
        step *= 2
    total = total * (1.0 / math.sqrt(nodes * blks))
    return (output, propagated, total[:, :width].T, total[:, width])


def solution(mesh):
    placed = (
        P(None, "blk"),
        P(),
        P("help"),
        P("help", "blk"),
        P("blk", "help", None, None, None),
        P("blk", "help", None),
        P("blk", "help", None),
    )
    return jax.shard_map(
        per_device,
        mesh=mesh,
        in_specs=placed,
        out_specs=(P("help", "blk"), P("help", "blk"), P(None, "help"), P("help")),
        check_vma=False,
    )
```

```python
import functools
import math

import jax
import jax.numpy as jnp
from jax import lax
from jax.experimental import pallas as pl
from jax.experimental.pallas import tpu as pltpu
from jax.sharding import PartitionSpec as P

BAND = 2
AXES = ("blk", "help")
ANY = pl.BlockSpec(memory_space=pl.ANY)
VMEM = pl.BlockSpec(memory_space=pltpu.VMEM)
SMEM = pl.BlockSpec(memory_space=pltpu.SMEM)
NT = (((1,), (1,)), ((), ()))
NN = (((1,), (0,)), ((), ()))
TN = (((0,), (0,)), ((), ()))


def move(block, source):
    blks, helps = lax.axis_size("blk"), lax.axis_size("help")
    route = []
    for b in range(blks):
        for h in range(helps):
            sb, sh = source(b, h)
            route.append(((sb % blks) * helps + sh, b * helps + h))
    return lax.ppermute(block, AXES, route)


def step_two(b, h, sign, blks):
    other = (b + 2 * sign) % blks
    half = blks // 2
    return (other, h if other // half == b // half else h ^ 1)


def window(block):
    blks = lax.axis_size("blk")
    swap = lambda b, h: (b ^ 1, h)
    one = move(block, lambda b, h: step_two(b, h, 1 if b % 2 == 0 else -1, blks))
    zero = move(block, swap)
    two = move(block, lambda b, h: step_two(b, h, -1 if b % 2 == 0 else 1, blks))
    three = move(one, swap)
    return (block, zero, one, two, three)


def load_all(refs, places, sems):
    copies = [
        pltpu.make_async_copy(ref, place, sems.at[i])
        for i, (ref, place) in enumerate(zip(refs, places))
    ]
    for copy in copies:
        copy.start()
    return copies


def add_pairs(pairs, rows, tiles, acc, piece, axis, dims):
    tile = tiles.shape[1]
    count = rows.shape[0]
    unroll = count // 2

    @pl.loop(0, count // unroll)
    def _(step):
        for j in range(unroll):
            i = step * unroll + j
            one, two = pairs[2 * i], pairs[2 * i + 1]
            left = jnp.concatenate([tiles[one & 127], tiles[two & 127]], axis=1)
            right = jnp.concatenate(
                [piece(pl.multiple_of((s >> 7) * tile, tile)) for s in (one, two)], axis=axis
            )
            product = lax.dot_general(left, right, dims, preferred_element_type=jnp.float32)
            acc[pl.ds(pl.multiple_of(rows[i] * tile, tile), tile), :] += product


def forward_kernel(pairs, rows, b0, b1, b2, b3, b4, tiles, cot, bias, out, win, acc, sems, stage, out_sems):
    tile = tiles.shape[1]
    nodes = cot.shape[1]
    refs = (b0, b1, b2, b3, b4)
    copies = load_all(refs, [win.at[:, i * nodes : (i + 1) * nodes] for i in range(5)], sems)
    acc[...] = jnp.zeros_like(acc)
    win[:, 5 * nodes :] = jnp.zeros((win.shape[0], tile), jnp.bfloat16)
    mine = nodes // out.shape[0]
    share = cot.shape[0]
    high = bias[...].astype(jnp.bfloat16)
    rest = bias[...] - high.astype(jnp.float32)
    middle = rest.astype(jnp.bfloat16)
    low = (rest - middle.astype(jnp.float32)).astype(jnp.bfloat16)
    lane = lax.broadcasted_iota(jnp.int32, (share, out.shape[2] - mine), 1)
    parts = jnp.where(lane == 0, high, jnp.where(lane == 1, middle, low))
    for h in range(out.shape[0]):
        stage[h, mine:, :mine] = cot[:, h * mine : (h + 1) * mine]
        stage[h, mine:, mine:] = parts
    for copy in copies:
        copy.wait()
    add_pairs(pairs, rows, tiles, acc, lambda c: win[:, pl.ds(c, tile)], 1, NT)
    leaving = []
    for h in range(out.shape[0]):
        stage[h, :mine, :] = acc[h * mine : (h + 1) * mine, :].astype(jnp.bfloat16)
        leaving.append(pltpu.make_async_copy(stage.at[h], out.at[h], out_sems.at[h]))
        leaving[h].start()
    for copy in leaving:
        copy.wait()


def backward_kernel(pairs, rows, b0, b1, b2, b3, b4, tiles, out, win, acc, sems, stage, out_sems):
    tile = tiles.shape[1]
    helps, share, nodes = out.shape
    width = helps * share
    refs = (b0, b1, b2, b3, b4)
    copies = load_all(refs, [win.at[i * nodes : (i + 1) * nodes, :] for i in range(5)], sems)
    acc[...] = jnp.zeros_like(acc)
    win[5 * nodes :, :] = jnp.zeros((tile, win.shape[1]), jnp.bfloat16)
    for copy in copies:
        copy.wait()
    add_pairs(pairs, rows, tiles, acc, lambda c: win[pl.ds(c, tile), :], 0, NN)
    eye = (
        lax.broadcasted_iota(jnp.int32, (width, width), 0)
        == lax.broadcasted_iota(jnp.int32, (width, width), 1)
    ).astype(jnp.bfloat16)
    for t in range(nodes // tile):
        part = acc[t * tile : (t + 1) * tile, :].astype(jnp.bfloat16)
        turned = lax.dot_general(eye, part, NT, preferred_element_type=jnp.float32)
        stage[:, :, t * tile : (t + 1) * tile] = turned.astype(jnp.bfloat16).reshape(helps, share, tile)
    leaving = [pltpu.make_async_copy(stage.at[h], out.at[h], out_sems.at[h]) for h in range(helps)]
    for copy in leaving:
        copy.start()
    for copy in leaving:
        copy.wait()


def aggregate(kernel, blocks, tiles, slots, out_shape, *extra):
    count, tile = tiles.shape[0], tiles.shape[1]
    nodes = max(blocks[0].shape)
    width = min(blocks[0].shape)
    forward = blocks[0].shape[1] == nodes
    span = 5 * nodes + tile
    parts = out_shape[0]
    return pl.pallas_call(
        kernel,
        out_shape=pltpu.HBM(out_shape, jnp.bfloat16),
        in_specs=[SMEM] * 2 + [ANY] * 5 + [VMEM] * (1 + len(extra)),
        out_specs=ANY,
        scratch_shapes=[
            pltpu.VMEM((width, span) if forward else (span, width), jnp.bfloat16),
            pltpu.VMEM((nodes + tile, width), jnp.float32),
            pltpu.SemaphoreType.DMA((5,)),
            pltpu.VMEM(out_shape, jnp.bfloat16),
            pltpu.SemaphoreType.DMA((parts,)),
        ],
        compiler_params=pltpu.CompilerParams(vmem_limit_bytes=20 * 2**20),
        cost_estimate=pl.CostEstimate(
            flops=2 * count * tile * tile * width,
            bytes_accessed=6 * 2**20,
            transcendentals=0,
        ),
    )(*slots, *blocks, tiles, *extra)


def prepare_kernel(row_tiles, odd, rows, cols, tiles, cot, own, pairs, heads, tiles_v, cot_v, own_v, following, sems):
    copies = load_all((tiles, cot, own), (tiles_v, cot_v, own_v), sems)
    spans = 2 * BAND + 1
    count = rows.shape[0]
    for r in range(row_tiles + 1):
        following[r] = 0

    @pl.loop(0, count, unroll=4)
    def _(k):
        r = rows[k]
        following[r] = following[r] + 1

    first = jnp.int32(0)
    for r in range(row_tiles):
        used = following[r]
        following[r] = first
        first = first + ((used + 1) >> 1) * 2
    following[row_tiles] = jnp.int32(pairs.shape[0])

    @pl.loop(0, heads.shape[0], unroll=4)
    def _(i):
        heads[i] = row_tiles
        pairs[2 * i] = 128 * spans * row_tiles
        pairs[2 * i + 1] = 128 * spans * row_tiles

    swapped = odd[0] == 1

    @pl.loop(0, count, unroll=4)
    def _(k):
        r = rows[k]
        place = following[r]
        following[r] = place + 1
        span = jnp.int32(0)
        for s in range(1, spans):
            span = span + (cols[k] >= s * row_tiles).astype(jnp.int32)
        even = jnp.where(span >= 2, span - 2, span + 3)
        other = jnp.where(span <= 2, 2 - span, 7 - span)
        buf = jnp.where(swapped, other, even)
        flat = buf * row_tiles + cols[k] - span * row_tiles

        @pl.when(r < row_tiles)
        def _():
            pairs[place] = k + 128 * flat
            heads[place >> 1] = r

    for copy in copies:
        copy.wait()


def middle_kernel(parts, weight_t, back, side):
    mine = back.shape[1]
    total = parts[0, :mine].astype(jnp.float32)
    for s in range(1, parts.shape[0]):
        total = total + parts[s, :mine].astype(jnp.float32)
    agg = total.astype(jnp.bfloat16)
    cotb = jnp.concatenate([parts[s, mine:] for s in range(parts.shape[0])], axis=0)
    extra = cotb[:, mine : mine + 64].astype(jnp.float32)
    bias = extra[:, 0:1] + extra[:, 1:2] + extra[:, 2:3]
    pre = lax.dot_general(weight_t[...], agg, NT, preferred_element_type=jnp.float32) + bias
    decay = jnp.exp(jnp.minimum(pre, 0.0))
    slope = jnp.where(pre > 0.0, 1.0, decay)
    grad = (cotb[:, :mine].astype(jnp.float32) * slope).astype(jnp.bfloat16)
    back_n = lax.dot_general(
        grad, weight_t[...], TN, preferred_element_type=jnp.float32
    ).astype(jnp.bfloat16)
    for s in range(back.shape[0]):
        back[s] = back_n
    width = agg.shape[1]
    side[:, :width] = lax.dot_general(
        grad, agg, NN, preferred_element_type=jnp.float32
    ).astype(jnp.bfloat16)
    side[:, width : width + mine] = jnp.where(pre > 0.0, pre, decay - 1.0).astype(jnp.bfloat16)
    rest = side.shape[1] - width - mine
    sums = jnp.sum(grad.astype(jnp.float32), axis=1, keepdims=True)
    high = sums.astype(jnp.bfloat16)
    low = (sums - high.astype(jnp.float32)).astype(jnp.bfloat16)
    lane = lax.broadcasted_iota(jnp.int32, (width, rest), 1)
    side[:, width + mine :] = jnp.where(lane == 0, high, low)


def side_kernel(parts, out, total):
    width = total.shape[1] - 128
    nodes = out.shape[1] // parts.shape[0]
    sums = parts[0].astype(jnp.float32)
    for s in range(1, parts.shape[0]):
        sums = sums + parts[s].astype(jnp.float32)
    for s in range(parts.shape[0]):
        out[:, s * nodes : (s + 1) * nodes] = parts[s, :, width : width + nodes]
    total[:, :width] = sums[:, :width]
    at = width + nodes
    both = sums[:, at : at + 1] + sums[:, at + 1 : at + 2]
    total[:, width:] = jnp.broadcast_to(both, (total.shape[0], 128))


def spread(x):
    return lax.all_to_all(x, "help", 0, 0)


def small_call(kernel, outs, *args):
    return pl.pallas_call(
        kernel,
        out_shape=tuple(jax.ShapeDtypeStruct(*o) for o in outs),
        in_specs=[VMEM] * len(args),
        out_specs=(VMEM,) * len(outs),
        compiler_params=pltpu.CompilerParams(vmem_limit_bytes=16 * 2**20),
    )(*args)


def after(value, other):
    return lax.optimization_barrier((value, other))[0]


def per_device(features_t, weight, bias, cotangent_t, tile_vals, slot_row, slot_col):
    tiles = tile_vals[0, 0]
    tile = tiles.shape[-1]
    width, nodes = features_t.shape
    row_tiles = nodes // tile
    helps = lax.axis_size("help")
    blks = lax.axis_size("blk")
    share = cotangent_t.shape[0]
    mine = nodes // helps
    count = tiles.shape[0]

    pair_count = (count + row_tiles + 3) // 4 * 2
    own = features_t
    around = window(own)[1:]
    pairs, heads, tiles, cot, own = pl.pallas_call(
        functools.partial(prepare_kernel, row_tiles),
        out_shape=(
            jax.ShapeDtypeStruct((2 * pair_count,), jnp.int32),
            jax.ShapeDtypeStruct((pair_count,), jnp.int32),
            pltpu.VMEM(tiles.shape, jnp.bfloat16),
            pltpu.VMEM(cotangent_t.shape, jnp.bfloat16),
            pltpu.VMEM(own.shape, jnp.bfloat16),
        ),
        in_specs=[SMEM] * 3 + [ANY] * 3,
        out_specs=(SMEM,) * 2 + (ANY,) * 3,
        scratch_shapes=[pltpu.SMEM((row_tiles + 1,), jnp.int32), pltpu.SemaphoreType.DMA((3,))],
        compiler_params=pltpu.CompilerParams(vmem_limit_bytes=2 * 2**20),
    )(
        (lax.axis_index("blk") % 2).astype(jnp.int32).reshape(1),
        slot_row[0, 0],
        slot_col[0, 0],
        tiles,
        cotangent_t,
        own,
    )
    slots = (pairs, heads)

    sent = aggregate(
        forward_kernel,
        (own, *around),
        tiles,
        slots,
        (helps, mine + share, width),
        cot,
        bias.reshape(share, 1),
    )
    back, side = small_call(
        middle_kernel,
        [((helps, mine, width), jnp.bfloat16), ((width, 2 * width), jnp.bfloat16)],
        spread(sent),
        weight.T,
    )
    back_full = spread(back).reshape(nodes, width)
    blocks = window(back_full)
    value = aggregate(backward_kernel, blocks, tiles, slots, (helps, share, nodes))
    summed = spread(value)
    propagated = jnp.sum(summed.astype(jnp.float32), axis=0)

    side = after(side.reshape(helps, share, 2 * width), back_full)
    output, total = small_call(
        side_kernel,
        [((share, nodes), jnp.bfloat16), ((share, width + tile), jnp.float32)],
        spread(side),
    )
    flip = lambda s: functools.partial(lambda s, b, h: (b ^ s, h), s)
    total = (total + move(total, flip(1))) + (
        move(total, flip(blks // 2)) + move(total, flip(blks // 2 + 1))
    )
    step = 2
    while step < blks // 2:
        if step == blks // 8:
            total = after(total, blocks[3])
        if step == blks // 4:
            total = after(total, value)
        total = total + move(total, flip(step))
        step *= 2
    total = total * (1.0 / math.sqrt(nodes * blks))
    return (output, propagated, total[:, :width].T, total[:, width])


def solution(mesh):
    placed = (
        P(None, "blk"),
        P(),
        P("help"),
        P("help", "blk"),
        P("blk", "help", None, None, None),
        P("blk", "help", None),
        P("blk", "help", None),
    )
    return jax.shard_map(
        per_device,
        mesh=mesh,
        in_specs=placed,
        out_specs=(P("help", "blk"), P("help", "blk"), P(None, "help"), P("help")),
        check_vma=False,
    )
```

```python
import functools
import math

import jax
import jax.numpy as jnp
from jax import lax
from jax.experimental import pallas as pl
from jax.experimental.pallas import tpu as pltpu
from jax.sharding import PartitionSpec as P

BAND = 2
AXES = ("blk", "help")
ANY = pl.BlockSpec(memory_space=pl.ANY)
VMEM = pl.BlockSpec(memory_space=pltpu.VMEM)
SMEM = pl.BlockSpec(memory_space=pltpu.SMEM)
NT = (((1,), (1,)), ((), ()))
NN = (((1,), (0,)), ((), ()))
TN = (((0,), (0,)), ((), ()))


def move(block, source):
    blks, helps = lax.axis_size("blk"), lax.axis_size("help")
    route = []
    for b in range(blks):
        for h in range(helps):
            sb, sh = source(b, h)
            route.append(((sb % blks) * helps + sh, b * helps + h))
    return lax.ppermute(block, AXES, route)


def step_two(b, h, sign, blks):
    other = (b + 2 * sign) % blks
    half = blks // 2
    return (other, h if other // half == b // half else h ^ 1)


def after(value, other):
    return lax.optimization_barrier((value, other))[0]


def near(block):
    blks = lax.axis_size("blk")
    one = move(block, lambda b, h: step_two(b, h, 1 if b % 2 == 0 else -1, blks))
    zero = move(block, lambda b, h: (b ^ 1, h))
    two = move(block, lambda b, h: step_two(b, h, -1 if b % 2 == 0 else 1, blks))
    return zero, one, two


def load_all(refs, places, sems):
    copies = [
        pltpu.make_async_copy(ref, place, sems.at[i])
        for i, (ref, place) in enumerate(zip(refs, places))
    ]
    for copy in copies:
        copy.start()
    return copies


def add_pairs(pairs, rows, tiles, acc, piece, axis, dims):
    tile = tiles.shape[1]
    count = rows.shape[0]
    unroll = count // 2

    @pl.loop(0, count // unroll)
    def _(step):
        for j in range(unroll):
            i = step * unroll + j
            one, two = pairs[2 * i], pairs[2 * i + 1]
            left = jnp.concatenate([tiles[one & 127], tiles[two & 127]], axis=1)
            right = jnp.concatenate(
                [piece(pl.multiple_of((s >> 7) * tile, tile)) for s in (one, two)], axis=axis
            )
            product = lax.dot_general(left, right, dims, preferred_element_type=jnp.float32)
            acc[pl.ds(pl.multiple_of(rows[i] * tile, tile), tile), :] += product


def forward_kernel(pairs, rows, b0, b1, b2, b3, b4, tiles, extra, out, win, acc, sems, stage, out_sems):
    tile = tiles.shape[1]
    nodes = b0.shape[1]
    helps = out.shape[0]
    mine = nodes // helps
    refs = (b0, b1, b2, b3, b4)
    copies = load_all(refs, [win.at[:, i * nodes : (i + 1) * nodes] for i in range(5)], sems)
    leaving = []
    for h in range(helps):
        leaving.append(pltpu.make_async_copy(extra.at[h], out.at[h, mine:], out_sems.at[helps + h]))
        leaving[h].start()
    acc[...] = jnp.zeros_like(acc)
    win[:, 5 * nodes :] = jnp.zeros((win.shape[0], tile), jnp.bfloat16)
    for copy in copies:
        copy.wait()
    add_pairs(pairs, rows, tiles, acc, lambda c: win[:, pl.ds(c, tile)], 1, NT)
    for h in range(helps):
        stage[h] = acc[h * mine : (h + 1) * mine, :].astype(jnp.bfloat16)
        leaving.append(pltpu.make_async_copy(stage.at[h], out.at[h, :mine], out_sems.at[h]))
        leaving[helps + h].start()
    for copy in leaving:
        copy.wait()


def backward_kernel(pairs, rows, b0, b1, b2, b3, b4, tiles, out, win, acc, sems, stage, out_sems):
    tile = tiles.shape[1]
    helps, share, nodes = out.shape
    width = helps * share
    refs = (b0, b1, b2, b3, b4)
    copies = load_all(refs, [win.at[i * nodes : (i + 1) * nodes, :] for i in range(5)], sems)
    acc[...] = jnp.zeros_like(acc)
    win[5 * nodes :, :] = jnp.zeros((tile, win.shape[1]), jnp.bfloat16)
    for copy in copies:
        copy.wait()
    add_pairs(pairs, rows, tiles, acc, lambda c: win[pl.ds(c, tile), :], 0, NN)
    eye = (
        lax.broadcasted_iota(jnp.int32, (width, width), 0)
        == lax.broadcasted_iota(jnp.int32, (width, width), 1)
    ).astype(jnp.bfloat16)
    for t in range(nodes // tile):
        part = acc[t * tile : (t + 1) * tile, :].astype(jnp.bfloat16)
        turned = lax.dot_general(eye, part, NT, preferred_element_type=jnp.float32)
        stage[:, :, t * tile : (t + 1) * tile] = turned.astype(jnp.bfloat16).reshape(helps, share, tile)
    leaving = [pltpu.make_async_copy(stage.at[h], out.at[h], out_sems.at[h]) for h in range(helps)]
    for copy in leaving:
        copy.start()
    for copy in leaving:
        copy.wait()


def aggregate(kernel, blocks, tiles, slots, out_shape, *extra):
    count, tile = tiles.shape[0], tiles.shape[1]
    nodes = max(blocks[0].shape)
    width = min(blocks[0].shape)
    forward = blocks[0].shape[1] == nodes
    span = 5 * nodes + tile
    parts = out_shape[0]
    return pl.pallas_call(
        kernel,
        out_shape=pltpu.HBM(out_shape, jnp.bfloat16),
        in_specs=[SMEM] * 2 + [ANY] * 5 + [VMEM] + [ANY] * len(extra),
        out_specs=ANY,
        scratch_shapes=[
            pltpu.VMEM((width, span) if forward else (span, width), jnp.bfloat16),
            pltpu.VMEM((nodes + tile, width), jnp.float32),
            pltpu.SemaphoreType.DMA((5,)),
            pltpu.VMEM((parts, nodes // parts, width) if forward else out_shape, jnp.bfloat16),
            pltpu.SemaphoreType.DMA((2 * parts,)),
        ],
        compiler_params=pltpu.CompilerParams(vmem_limit_bytes=20 * 2**20),
        cost_estimate=pl.CostEstimate(
            flops=2 * count * tile * tile * width,
            bytes_accessed=6 * 2**20,
            transcendentals=0,
        ),
    )(*slots, *blocks, tiles, *extra)


def prepare_kernel(row_tiles, odd, rows, cols, bias, tiles, cot, own, pairs, heads, extra, tiles_v, own_v, following, cot_v, sems):
    copies = load_all((tiles, cot, own), (tiles_v, cot_v, own_v), sems)
    spans = 2 * BAND + 1
    count = rows.shape[0]
    for r in range(row_tiles + 1):
        following[r] = 0

    @pl.loop(0, count, unroll=4)
    def _(k):
        r = rows[k]
        following[r] = following[r] + 1

    first = jnp.int32(0)
    for r in range(row_tiles):
        used = following[r]
        following[r] = first
        first = first + ((used + 1) >> 1) * 2
    following[row_tiles] = jnp.int32(pairs.shape[0])

    @pl.loop(0, heads.shape[0], unroll=4)
    def _(i):
        heads[i] = row_tiles
        pairs[2 * i] = 128 * spans * row_tiles
        pairs[2 * i + 1] = 128 * spans * row_tiles

    swapped = odd[0] == 1

    @pl.loop(0, count, unroll=4)
    def _(k):
        r = rows[k]
        place = following[r]
        following[r] = place + 1
        span = jnp.int32(0)
        for s in range(1, spans):
            span = span + (cols[k] >= s * row_tiles).astype(jnp.int32)
        even = jnp.where(span >= 2, span - 2, span + 3)
        other = jnp.where(span <= 2, 2 - span, 7 - span)
        buf = jnp.where(swapped, other, even)
        flat = buf * row_tiles + cols[k] - span * row_tiles

        @pl.when(r < row_tiles)
        def _():
            pairs[place] = k + 128 * flat
            heads[place >> 1] = r

    helps, share, lanes = extra.shape
    mine = cot_v.shape[1] // helps
    high = bias[...].astype(jnp.bfloat16)
    rest = bias[...] - high.astype(jnp.float32)
    middle = rest.astype(jnp.bfloat16)
    low = (rest - middle.astype(jnp.float32)).astype(jnp.bfloat16)
    lane = lax.broadcasted_iota(jnp.int32, (share, lanes - mine), 1)
    bias_parts = jnp.where(lane == 0, high, jnp.where(lane == 1, middle, low))
    for copy in copies:
        copy.wait()
    for h in range(helps):
        extra[h, :, :mine] = cot_v[:, h * mine : (h + 1) * mine]
        extra[h, :, mine:] = bias_parts


def middle_kernel(parts, weight_t, out):
    helps, length, width = out.shape
    share = width // helps
    mine = length - 2 * share
    total = parts[0, :mine].astype(jnp.float32)
    for s in range(1, helps):
        total = total + parts[s, :mine].astype(jnp.float32)
    agg = total.astype(jnp.bfloat16)
    cotb = jnp.concatenate([parts[s, mine:] for s in range(helps)], axis=0)
    extra = cotb[:, mine:].astype(jnp.float32)
    bias = extra[:, 0:1] + extra[:, 1:2] + extra[:, 2:3]
    pre = lax.dot_general(weight_t[...], agg, NT, preferred_element_type=jnp.float32) + bias
    decay = jnp.exp(jnp.minimum(pre, 0.0))
    slope = jnp.where(pre > 0.0, 1.0, decay)
    grad = (cotb[:, :mine].astype(jnp.float32) * slope).astype(jnp.bfloat16)
    back = lax.dot_general(
        grad, weight_t[...], TN, preferred_element_type=jnp.float32
    ).astype(jnp.bfloat16)
    terms = lax.dot_general(grad, agg, NN, preferred_element_type=jnp.float32).astype(jnp.bfloat16)
    result = jnp.where(pre > 0.0, pre, decay - 1.0).astype(jnp.bfloat16)
    sums = jnp.sum(grad.astype(jnp.float32), axis=1, keepdims=True)
    high = sums.astype(jnp.bfloat16)
    low = (sums - high.astype(jnp.float32)).astype(jnp.bfloat16)
    lane = lax.broadcasted_iota(jnp.int32, (width, width - mine), 1)
    sums = jnp.where(lane == 0, high, low)
    for h in range(helps):
        own = slice(h * share, (h + 1) * share)
        out[h, :mine, :] = back
        out[h, mine : mine + share, :] = terms[own]
        out[h, mine + share :, :mine] = result[own]
        out[h, mine + share :, mine:] = sums[own]


def divide_kernel(parts, back, out, total, side, sems):
    helps, _, width = parts.shape
    mine = back.shape[0] // helps
    share = total.shape[0]
    copies = []
    for s in range(helps):
        copies.append(pltpu.make_async_copy(parts.at[s, mine:], side.at[s], sems.at[s]))
        copies.append(
            pltpu.make_async_copy(
                parts.at[s, :mine], back.at[s * mine : (s + 1) * mine], sems.at[helps + s]
            )
        )
    for copy in copies:
        copy.start()
    for copy in copies[0::2]:
        copy.wait()
    sums = side[0].astype(jnp.float32)
    for s in range(1, helps):
        sums = sums + side[s].astype(jnp.float32)
    total[:, :width] = sums[:share]
    both = sums[share:, mine : mine + 1] + sums[share:, mine + 1 : mine + 2]
    total[:, width:] = jnp.broadcast_to(both, (share, total.shape[1] - width))
    for s in range(helps):
        out[:, s * mine : (s + 1) * mine] = side[s, share:, :mine]
    for copy in copies[1::2]:
        copy.wait()


def spread(x):
    return lax.all_to_all(x, "help", 0, 0)


def round_of_four(total, one, two):
    got = [
        move(total, functools.partial(lambda s, b, h: (b ^ s, h), s)) for s in (one, two, one ^ two)
    ]
    return (total + got[0]) + (got[1] + got[2])


def per_device(features_t, weight, bias, cotangent_t, tile_vals, slot_row, slot_col):
    tiles = tile_vals[0, 0]
    tile = tiles.shape[-1]
    width, nodes = features_t.shape
    row_tiles = nodes // tile
    helps = lax.axis_size("help")
    blks = lax.axis_size("blk")
    share = cotangent_t.shape[0]
    mine = nodes // helps
    count = tiles.shape[0]
    swap = lambda b, h: (b ^ 1, h)

    zero, one, two = near(features_t)
    pair_count = (count + row_tiles + 3) // 4 * 2
    pairs, heads, extra, tiles, own = pl.pallas_call(
        functools.partial(prepare_kernel, row_tiles),
        out_shape=(
            jax.ShapeDtypeStruct((2 * pair_count,), jnp.int32),
            jax.ShapeDtypeStruct((pair_count,), jnp.int32),
            jax.ShapeDtypeStruct((helps, share, width), jnp.bfloat16),
            pltpu.VMEM(tiles.shape, jnp.bfloat16),
            pltpu.VMEM(features_t.shape, jnp.bfloat16),
        ),
        in_specs=[SMEM] * 3 + [VMEM] + [ANY] * 3,
        out_specs=(SMEM,) * 2 + (VMEM,) + (ANY,) * 2,
        scratch_shapes=[
            pltpu.SMEM((row_tiles + 1,), jnp.int32),
            pltpu.VMEM(cotangent_t.shape, jnp.bfloat16),
            pltpu.SemaphoreType.DMA((3,)),
        ],
        compiler_params=pltpu.CompilerParams(vmem_limit_bytes=4 * 2**20),
    )(
        (lax.axis_index("blk") % 2).astype(jnp.int32).reshape(1),
        slot_row[0, 0],
        slot_col[0, 0],
        bias.reshape(share, 1),
        tiles,
        cotangent_t,
        features_t,
    )
    slots = (pairs, heads)
    three = move(after(one, own), swap)
    sent = aggregate(
        forward_kernel,
        (own, zero, one, two, three),
        tiles,
        slots,
        (helps, mine + share, width),
        extra,
    )
    length = mine + 2 * share
    sent = pl.pallas_call(
        middle_kernel,
        out_shape=jax.ShapeDtypeStruct((helps, length, width), jnp.bfloat16),
        in_specs=[VMEM] * 2,
        out_specs=VMEM,
        compiler_params=pltpu.CompilerParams(vmem_limit_bytes=16 * 2**20),
    )(spread(sent), weight.T)
    back, output, total = pl.pallas_call(
        divide_kernel,
        out_shape=(
            pltpu.VMEM((nodes, width), jnp.bfloat16),
            jax.ShapeDtypeStruct((share, nodes), jnp.bfloat16),
            jax.ShapeDtypeStruct((share, width + tile), jnp.float32),
        ),
        in_specs=[ANY],
        out_specs=(ANY, VMEM, VMEM),
        scratch_shapes=[
            pltpu.VMEM((helps, 2 * share, width), jnp.bfloat16),
            pltpu.SemaphoreType.DMA((2 * helps,)),
        ],
        compiler_params=pltpu.CompilerParams(vmem_limit_bytes=4 * 2**20),
    )(spread(sent))
    zero, one, two = near(back)
    half = blks // 2
    total = round_of_four(total, 1, half)
    total = round_of_four(total, 2, 4)
    three = move(after(one, (total, two)), swap)
    value = aggregate(
        backward_kernel, (back, zero, one, two, three), tiles, slots, (helps, share, nodes)
    )
    propagated = jnp.sum(spread(value).astype(jnp.float32), axis=0)
    total = round_of_four(total, 8, 16)
    total = total * (1.0 / math.sqrt(nodes * blks))
    return (output, propagated, total[:, :width].T, total[:, width])


def solution(mesh):
    placed = (
        P(None, "blk"),
        P(),
        P("help"),
        P("help", "blk"),
        P("blk", "help", None, None, None),
        P("blk", "help", None),
        P("blk", "help", None),
    )
    return jax.shard_map(
        per_device,
        mesh=mesh,
        in_specs=placed,
        out_specs=(P("help", "blk"), P("help", "blk"), P(None, "help"), P("help")),
        check_vma=False,
    )
```

```python
import functools
import math

import jax
import jax.numpy as jnp
from jax import lax
from jax.experimental import pallas as pl
from jax.experimental.pallas import tpu as pltpu
from jax.sharding import PartitionSpec as P

BAND = 2
AXES = ("blk", "help")
ANY = pl.BlockSpec(memory_space=pl.ANY)
VMEM = pl.BlockSpec(memory_space=pltpu.VMEM)
SMEM = pl.BlockSpec(memory_space=pltpu.SMEM)
NT = (((1,), (1,)), ((), ()))
NN = (((1,), (0,)), ((), ()))
TN = (((0,), (0,)), ((), ()))


def move(block, source):
    blks, helps = lax.axis_size("blk"), lax.axis_size("help")
    route = []
    for b in range(blks):
        for h in range(helps):
            sb, sh = source(b, h)
            route.append(((sb % blks) * helps + sh, b * helps + h))
    return lax.ppermute(block, AXES, route)


def step_two(b, h, sign, blks):
    other = (b + 2 * sign) % blks
    half = blks // 2
    return (other, h if other // half == b // half else h ^ 1)


def after(value, other):
    return lax.optimization_barrier((value, other))[0]


def near(block):
    blks = lax.axis_size("blk")
    one = move(block, lambda b, h: step_two(b, h, 1 if b % 2 == 0 else -1, blks))
    zero = move(block, lambda b, h: (b ^ 1, h))
    two = move(block, lambda b, h: step_two(b, h, -1 if b % 2 == 0 else 1, blks))
    return zero, one, two


def unit(size):
    place = (size, size)
    return (
        lax.broadcasted_iota(jnp.int32, place, 0) == lax.broadcasted_iota(jnp.int32, place, 1)
    ).astype(jnp.bfloat16)


def load_all(refs, places, sems):
    copies = [
        pltpu.make_async_copy(ref, place, sems.at[i])
        for i, (ref, place) in enumerate(zip(refs, places))
    ]
    for copy in copies:
        copy.start()
    return copies


def add_pairs(pairs, rows, tiles, acc, piece, axis, dims):
    tile = tiles.shape[1]
    count = rows.shape[0]
    unroll = count // 2

    @pl.loop(0, count // unroll)
    def _(step):
        for j in range(unroll):
            i = step * unroll + j
            one, two = pairs[2 * i], pairs[2 * i + 1]
            left = jnp.concatenate([tiles[one & 127], tiles[two & 127]], axis=1)
            right = jnp.concatenate(
                [piece(pl.multiple_of((s >> 7) * tile, tile)) for s in (one, two)], axis=axis
            )
            product = lax.dot_general(left, right, dims, preferred_element_type=jnp.float32)
            acc[pl.ds(pl.multiple_of(rows[i] * tile, tile), tile), :] += product


def forward_kernel(pairs, rows, b0, b1, b2, b3, b4, tiles, extra, out, win, acc, sems, stage, out_sems):
    tile = tiles.shape[1]
    nodes = b0.shape[1]
    helps = out.shape[0]
    mine = nodes // helps
    refs = (b0, b1, b2, b3, b4)
    copies = load_all(refs, [win.at[:, i * nodes : (i + 1) * nodes] for i in range(5)], sems)
    leaving = []
    for h in range(helps):
        leaving.append(pltpu.make_async_copy(extra.at[h], out.at[h, mine:], out_sems.at[helps + h]))
        leaving[h].start()
    acc[...] = jnp.zeros_like(acc)
    win[:, 5 * nodes :] = jnp.zeros((win.shape[0], tile), jnp.bfloat16)
    for copy in copies:
        copy.wait()
    add_pairs(pairs, rows, tiles, acc, lambda c: win[:, pl.ds(c, tile)], 1, NT)
    for h in range(helps):
        stage[h] = acc[h * mine : (h + 1) * mine, :].astype(jnp.bfloat16)
        leaving.append(pltpu.make_async_copy(stage.at[h], out.at[h, :mine], out_sems.at[h]))
        leaving[helps + h].start()
    for copy in leaving:
        copy.wait()


def backward_kernel(pairs, rows, b0, b1, b2, b3, b4, tiles, out, win, acc, sems, stage, out_sems):
    tile = tiles.shape[1]
    helps, share, nodes = out.shape
    width = helps * share
    refs = (b0, b1, b2, b3, b4)
    copies = load_all(refs, [win.at[i * nodes : (i + 1) * nodes, :] for i in range(5)], sems)
    acc[...] = jnp.zeros_like(acc)
    win[5 * nodes :, :] = jnp.zeros((tile, win.shape[1]), jnp.bfloat16)
    for copy in copies:
        copy.wait()
    add_pairs(pairs, rows, tiles, acc, lambda c: win[pl.ds(c, tile), :], 0, NN)
    eye = unit(width)
    for t in range(nodes // tile):
        part = acc[t * tile : (t + 1) * tile, :].astype(jnp.bfloat16)
        turned = lax.dot_general(eye, part, NT, preferred_element_type=jnp.float32)
        stage[:, :, t * tile : (t + 1) * tile] = turned.astype(jnp.bfloat16).reshape(helps, share, tile)
    leaving = [pltpu.make_async_copy(stage.at[h], out.at[h], out_sems.at[h]) for h in range(helps)]
    for copy in leaving:
        copy.start()
    for copy in leaving:
        copy.wait()


def aggregate(kernel, blocks, tiles, slots, out_shape, *extra):
    count, tile = tiles.shape[0], tiles.shape[1]
    nodes = max(blocks[0].shape)
    width = min(blocks[0].shape)
    forward = blocks[0].shape[1] == nodes
    span = 5 * nodes + tile
    parts = out_shape[0]
    return pl.pallas_call(
        kernel,
        out_shape=pltpu.HBM(out_shape, jnp.bfloat16),
        in_specs=[SMEM] * 2 + [ANY] * 5 + [VMEM] + [ANY] * len(extra),
        out_specs=ANY,
        scratch_shapes=[
            pltpu.VMEM((width, span) if forward else (span, width), jnp.bfloat16),
            pltpu.VMEM((nodes + tile, width), jnp.float32),
            pltpu.SemaphoreType.DMA((5,)),
            pltpu.VMEM((parts, nodes // parts, width) if forward else out_shape, jnp.bfloat16),
            pltpu.SemaphoreType.DMA((2 * parts,)),
        ],
        compiler_params=pltpu.CompilerParams(vmem_limit_bytes=20 * 2**20),
        cost_estimate=pl.CostEstimate(
            flops=2 * count * tile * tile * width,
            bytes_accessed=6 * 2**20,
            transcendentals=0,
        ),
    )(*slots, *blocks, tiles, *extra)


def prepare_kernel(row_tiles, odd, rows, cols, bias, weight, tiles, cot, own, pairs, heads, extra, weight_t, tiles_v, own_v, following, cot_v, sems):
    copies = load_all((tiles, cot, own), (tiles_v, cot_v, own_v), sems)
    weight_t[...] = lax.dot_general(
        unit(weight.shape[0]), weight[...], NT, preferred_element_type=jnp.float32
    ).astype(jnp.bfloat16)
    spans = 2 * BAND + 1
    count = rows.shape[0]
    for r in range(row_tiles + 1):
        following[r] = 0

    @pl.loop(0, count, unroll=4)
    def _(k):
        r = rows[k]
        following[r] = following[r] + 1

    first = jnp.int32(0)
    for r in range(row_tiles):
        used = following[r]
        following[r] = first
        first = first + ((used + 1) >> 1) * 2
    following[row_tiles] = jnp.int32(pairs.shape[0])

    @pl.loop(0, heads.shape[0], unroll=4)
    def _(i):
        heads[i] = row_tiles
        pairs[2 * i] = 128 * spans * row_tiles
        pairs[2 * i + 1] = 128 * spans * row_tiles

    swapped = odd[0] == 1

    @pl.loop(0, count, unroll=4)
    def _(k):
        r = rows[k]
        place = following[r]
        following[r] = place + 1
        span = jnp.int32(0)
        for s in range(1, spans):
            span = span + (cols[k] >= s * row_tiles).astype(jnp.int32)
        even = jnp.where(span >= 2, span - 2, span + 3)
        other = jnp.where(span <= 2, 2 - span, 7 - span)
        buf = jnp.where(swapped, other, even)
        flat = buf * row_tiles + cols[k] - span * row_tiles

        @pl.when(r < row_tiles)
        def _():
            pairs[place] = k + 128 * flat
            heads[place >> 1] = r

    helps, share, lanes = extra.shape
    mine = cot_v.shape[1] // helps
    high = bias[...].astype(jnp.bfloat16)
    rest = bias[...] - high.astype(jnp.float32)
    middle = rest.astype(jnp.bfloat16)
    low = (rest - middle.astype(jnp.float32)).astype(jnp.bfloat16)
    lane = lax.broadcasted_iota(jnp.int32, (share, lanes - mine), 1)
    bias_parts = jnp.where(lane == 0, high, jnp.where(lane == 1, middle, low))
    for copy in copies:
        copy.wait()
    for h in range(helps):
        extra[h, :, :mine] = cot_v[:, h * mine : (h + 1) * mine]
        extra[h, :, mine:] = bias_parts


def middle_kernel(parts, weight_t, out):
    helps, length, width = out.shape
    share = width // helps
    mine = length - 2 * share
    total = parts[0, :mine].astype(jnp.float32)
    for s in range(1, helps):
        total = total + parts[s, :mine].astype(jnp.float32)
    agg = total.astype(jnp.bfloat16)
    cotb = jnp.concatenate([parts[s, mine:] for s in range(helps)], axis=0)
    extra = cotb[:, mine:].astype(jnp.float32)
    bias = extra[:, 0:1] + extra[:, 1:2] + extra[:, 2:3]
    pre = lax.dot_general(weight_t[...], agg, NT, preferred_element_type=jnp.float32) + bias
    decay = jnp.exp(jnp.minimum(pre, 0.0))
    slope = jnp.where(pre > 0.0, 1.0, decay)
    grad = (cotb[:, :mine].astype(jnp.float32) * slope).astype(jnp.bfloat16)
    back = lax.dot_general(
        grad, weight_t[...], TN, preferred_element_type=jnp.float32
    ).astype(jnp.bfloat16)
    terms = lax.dot_general(grad, agg, NN, preferred_element_type=jnp.float32).astype(jnp.bfloat16)
    result = jnp.where(pre > 0.0, pre, decay - 1.0).astype(jnp.bfloat16)
    sums = jnp.sum(grad.astype(jnp.float32), axis=1, keepdims=True)
    high = sums.astype(jnp.bfloat16)
    low = (sums - high.astype(jnp.float32)).astype(jnp.bfloat16)
    lane = lax.broadcasted_iota(jnp.int32, (width, width - mine), 1)
    sums = jnp.where(lane == 0, high, low)
    for h in range(helps):
        own = slice(h * share, (h + 1) * share)
        out[h, :mine, :] = back
        out[h, mine : mine + share, :] = terms[own]
        out[h, mine + share :, :mine] = result[own]
        out[h, mine + share :, mine:] = sums[own]


def divide_kernel(parts, back, out, total, side, sems):
    helps, _, width = parts.shape
    mine = back.shape[0] // helps
    share = total.shape[0]
    copies = []
    for s in range(helps):
        copies.append(pltpu.make_async_copy(parts.at[s, mine:], side.at[s], sems.at[s]))
        copies.append(
            pltpu.make_async_copy(
                parts.at[s, :mine], back.at[s * mine : (s + 1) * mine], sems.at[helps + s]
            )
        )
    for copy in copies:
        copy.start()
    for copy in copies[0::2]:
        copy.wait()
    sums = side[0].astype(jnp.float32)
    for s in range(1, helps):
        sums = sums + side[s].astype(jnp.float32)
    total[:, :width] = sums[:share]
    both = sums[share:, mine : mine + 1] + sums[share:, mine + 1 : mine + 2]
    total[:, width:] = jnp.broadcast_to(both, (share, total.shape[1] - width))
    for s in range(helps):
        out[:, s * mine : (s + 1) * mine] = side[s, share:, :mine]
    for copy in copies[1::2]:
        copy.wait()


def spread(x):
    return lax.all_to_all(x, "help", 0, 0)


def round_of_four(total, one, two):
    got = [
        move(total, functools.partial(lambda s, b, h: (b ^ s, h), s)) for s in (one, two, one ^ two)
    ]
    return (total + got[0]) + (got[1] + got[2])


def per_device(features_t, weight, bias, cotangent_t, tile_vals, slot_row, slot_col):
    tiles = tile_vals[0, 0]
    tile = tiles.shape[-1]
    width, nodes = features_t.shape
    row_tiles = nodes // tile
    helps = lax.axis_size("help")
    blks = lax.axis_size("blk")
    share = cotangent_t.shape[0]
    mine = nodes // helps
    count = tiles.shape[0]
    swap = lambda b, h: (b ^ 1, h)

    zero, one, two = near(features_t)
    pair_count = (count + row_tiles + 3) // 4 * 2
    pairs, heads, extra, weight_t, tiles, own = pl.pallas_call(
        functools.partial(prepare_kernel, row_tiles),
        out_shape=(
            jax.ShapeDtypeStruct((2 * pair_count,), jnp.int32),
            jax.ShapeDtypeStruct((pair_count,), jnp.int32),
            jax.ShapeDtypeStruct((helps, share, width), jnp.bfloat16),
            jax.ShapeDtypeStruct(weight.shape, jnp.bfloat16),
            pltpu.VMEM(tiles.shape, jnp.bfloat16),
            pltpu.VMEM(features_t.shape, jnp.bfloat16),
        ),
        in_specs=[SMEM] * 3 + [VMEM] * 2 + [ANY] * 3,
        out_specs=(SMEM,) * 2 + (VMEM,) * 2 + (ANY,) * 2,
        scratch_shapes=[
            pltpu.SMEM((row_tiles + 1,), jnp.int32),
            pltpu.VMEM(cotangent_t.shape, jnp.bfloat16),
            pltpu.SemaphoreType.DMA((3,)),
        ],
        compiler_params=pltpu.CompilerParams(vmem_limit_bytes=4 * 2**20),
    )(
        (lax.axis_index("blk") % 2).astype(jnp.int32).reshape(1),
        slot_row[0, 0],
        slot_col[0, 0],
        bias.reshape(share, 1),
        weight,
        *(pltpu.with_memory_space_constraint(x, pltpu.HBM) for x in (tiles, cotangent_t, features_t)),
    )
    slots = (pairs, heads)
    three = move(after(one, own), swap)
    sent = aggregate(
        forward_kernel,
        (own, zero, one, two, three),
        tiles,
        slots,
        (helps, mine + share, width),
        extra,
    )
    length = mine + 2 * share
    sent = pl.pallas_call(
        middle_kernel,
        out_shape=jax.ShapeDtypeStruct((helps, length, width), jnp.bfloat16),
        in_specs=[VMEM] * 2,
        out_specs=VMEM,
        compiler_params=pltpu.CompilerParams(vmem_limit_bytes=16 * 2**20),
    )(spread(sent), weight_t)
    back, output, total = pl.pallas_call(
        divide_kernel,
        out_shape=(
            pltpu.VMEM((nodes, width), jnp.bfloat16),
            jax.ShapeDtypeStruct((share, nodes), jnp.bfloat16),
            jax.ShapeDtypeStruct((share, width + tile), jnp.float32),
        ),
        in_specs=[ANY],
        out_specs=(ANY, VMEM, VMEM),
        scratch_shapes=[
            pltpu.VMEM((helps, 2 * share, width), jnp.bfloat16),
            pltpu.SemaphoreType.DMA((2 * helps,)),
        ],
        compiler_params=pltpu.CompilerParams(vmem_limit_bytes=4 * 2**20),
    )(spread(sent))
    zero, one, two = near(back)
    half = blks // 2
    total = after(round_of_four(total, 1, half), two)
    three = move(after(one, total), swap)
    total = round_of_four(total, 8, 16)
    value = aggregate(
        backward_kernel, (back, zero, one, two, three), tiles, slots, (helps, share, nodes)
    )
    propagated = jnp.sum(spread(value).astype(jnp.float32), axis=0)
    total = round_of_four(total, 2, 4)
    total = total * (1.0 / math.sqrt(nodes * blks))
    return (output, propagated, total[:, :width].T, total[:, width])


def solution(mesh):
    placed = (
        P(None, "blk"),
        P(),
        P("help"),
        P("help", "blk"),
        P("blk", "help", None, None, None),
        P("blk", "help", None),
        P("blk", "help", None),
    )
    return jax.shard_map(
        per_device,
        mesh=mesh,
        in_specs=placed,
        out_specs=(P("help", "blk"), P("help", "blk"), P(None, "help"), P("help")),
        check_vma=False,
    )
```

```python
import functools
import math

import jax
import jax.numpy as jnp
from jax import lax
from jax.experimental import pallas as pl
from jax.experimental.pallas import tpu as pltpu
from jax.sharding import PartitionSpec as P

BAND = 2
AXES = ("blk", "help")
ANY = pl.BlockSpec(memory_space=pl.ANY)
VMEM = pl.BlockSpec(memory_space=pltpu.VMEM)
SMEM = pl.BlockSpec(memory_space=pltpu.SMEM)
NT = (((1,), (1,)), ((), ()))
NN = (((1,), (0,)), ((), ()))
TN = (((0,), (0,)), ((), ()))


def move(block, source):
    blks, helps = lax.axis_size("blk"), lax.axis_size("help")
    route = []
    for b in range(blks):
        for h in range(helps):
            sb, sh = source(b, h)
            route.append(((sb % blks) * helps + sh, b * helps + h))
    return lax.ppermute(block, AXES, route)


def step_two(b, h, sign, blks):
    other = (b + 2 * sign) % blks
    half = blks // 2
    return (other, h if other // half == b // half else h ^ 1)


def after(value, other):
    return lax.optimization_barrier((value, other))[0]


def near(block):
    blks = lax.axis_size("blk")
    one = move(block, lambda b, h: step_two(b, h, 1 if b % 2 == 0 else -1, blks))
    zero = move(block, lambda b, h: (b ^ 1, h))
    two = move(block, lambda b, h: step_two(b, h, -1 if b % 2 == 0 else 1, blks))
    return zero, one, two


def unit(size):
    place = (size, size)
    return (
        lax.broadcasted_iota(jnp.int32, place, 0) == lax.broadcasted_iota(jnp.int32, place, 1)
    ).astype(jnp.bfloat16)


def load_all(refs, places, sems):
    copies = [
        pltpu.make_async_copy(ref, place, sems.at[i])
        for i, (ref, place) in enumerate(zip(refs, places))
    ]
    for copy in copies:
        copy.start()
    return copies


def add_pairs(pairs, rows, tiles, acc, piece, axis, dims):
    tile = tiles.shape[1]
    count = rows.shape[0]
    unroll = count // 2

    @pl.loop(0, count // unroll)
    def _(step):
        for j in range(unroll):
            i = step * unroll + j
            one, two = pairs[2 * i], pairs[2 * i + 1]
            left = jnp.concatenate([tiles[one & 127], tiles[two & 127]], axis=1)
            right = jnp.concatenate(
                [piece(pl.multiple_of((s >> 7) * tile, tile)) for s in (one, two)], axis=axis
            )
            product = lax.dot_general(left, right, dims, preferred_element_type=jnp.float32)
            acc[pl.ds(pl.multiple_of(rows[i] * tile, tile), tile), :] += product


def forward_kernel(pairs, rows, b0, b1, b2, b3, b4, tiles, extra, out, win, acc, sems, stage, out_sems):
    tile = tiles.shape[1]
    nodes = b0.shape[1]
    helps = out.shape[0]
    mine = nodes // helps
    refs = (b0, b1, b2, b3, b4)
    copies = load_all(refs, [win.at[:, i * nodes : (i + 1) * nodes] for i in range(5)], sems)
    leaving = []
    for h in range(helps):
        leaving.append(pltpu.make_async_copy(extra.at[h], out.at[h, mine:], out_sems.at[helps + h]))
        leaving[h].start()
    acc[...] = jnp.zeros_like(acc)
    win[:, 5 * nodes :] = jnp.zeros((win.shape[0], tile), jnp.bfloat16)
    for copy in copies:
        copy.wait()
    add_pairs(pairs, rows, tiles, acc, lambda c: win[:, pl.ds(c, tile)], 1, NT)
    for h in range(helps):
        stage[h] = acc[h * mine : (h + 1) * mine, :].astype(jnp.bfloat16)
        leaving.append(pltpu.make_async_copy(stage.at[h], out.at[h, :mine], out_sems.at[h]))
        leaving[helps + h].start()
    for copy in leaving:
        copy.wait()


def backward_kernel(pairs, rows, b0, b1, b2, b3, b4, tiles, out, win, acc, sems, stage, out_sems):
    tile = tiles.shape[1]
    helps, share, nodes = out.shape
    width = helps * share
    refs = (b0, b1, b2, b3, b4)
    copies = load_all(refs, [win.at[i * nodes : (i + 1) * nodes, :] for i in range(5)], sems)
    acc[...] = jnp.zeros_like(acc)
    win[5 * nodes :, :] = jnp.zeros((tile, win.shape[1]), jnp.bfloat16)
    for copy in copies:
        copy.wait()
    add_pairs(pairs, rows, tiles, acc, lambda c: win[pl.ds(c, tile), :], 0, NN)
    eye = unit(width)
    for t in range(nodes // tile):
        part = acc[t * tile : (t + 1) * tile, :].astype(jnp.bfloat16)
        turned = lax.dot_general(eye, part, NT, preferred_element_type=jnp.float32)
        stage[:, :, t * tile : (t + 1) * tile] = turned.astype(jnp.bfloat16).reshape(helps, share, tile)
    leaving = [pltpu.make_async_copy(stage.at[h], out.at[h], out_sems.at[h]) for h in range(helps)]
    for copy in leaving:
        copy.start()
    for copy in leaving:
        copy.wait()


def aggregate(kernel, blocks, tiles, slots, out_shape, *extra):
    count, tile = tiles.shape[0], tiles.shape[1]
    nodes = max(blocks[0].shape)
    width = min(blocks[0].shape)
    forward = blocks[0].shape[1] == nodes
    span = 5 * nodes + tile
    parts = out_shape[0]
    return pl.pallas_call(
        kernel,
        out_shape=pltpu.HBM(out_shape, jnp.bfloat16),
        in_specs=[SMEM] * 2 + [ANY] * 5 + [VMEM] + [ANY] * len(extra),
        out_specs=ANY,
        scratch_shapes=[
            pltpu.VMEM((width, span) if forward else (span, width), jnp.bfloat16),
            pltpu.VMEM((nodes + tile, width), jnp.float32),
            pltpu.SemaphoreType.DMA((5,)),
            pltpu.VMEM((parts, nodes // parts, width) if forward else out_shape, jnp.bfloat16),
            pltpu.SemaphoreType.DMA((2 * parts,)),
        ],
        compiler_params=pltpu.CompilerParams(vmem_limit_bytes=20 * 2**20),
        cost_estimate=pl.CostEstimate(
            flops=2 * count * tile * tile * width,
            bytes_accessed=6 * 2**20,
            transcendentals=0,
        ),
    )(*slots, *blocks, tiles, *extra)


def prepare_kernel(row_tiles, odd, rows, cols, bias, weight, tiles, cot, own, pairs, heads, extra, weight_t, tiles_v, own_v, following, cot_v, sems):
    copies = load_all((tiles, cot, own), (tiles_v, cot_v, own_v), sems)
    weight_t[...] = lax.dot_general(
        unit(weight.shape[0]), weight[...], NT, preferred_element_type=jnp.float32
    ).astype(jnp.bfloat16)
    spans = 2 * BAND + 1
    count = rows.shape[0]
    for r in range(row_tiles + 1):
        following[r] = 0

    @pl.loop(0, count, unroll=4)
    def _(k):
        r = rows[k]
        following[r] = following[r] + 1

    first = jnp.int32(0)
    for r in range(row_tiles):
        used = following[r]
        following[r] = first
        first = first + ((used + 1) >> 1) * 2
    following[row_tiles] = jnp.int32(pairs.shape[0])

    @pl.loop(0, heads.shape[0], unroll=4)
    def _(i):
        heads[i] = row_tiles
        pairs[2 * i] = 128 * spans * row_tiles
        pairs[2 * i + 1] = 128 * spans * row_tiles

    swapped = odd[0] == 1

    @pl.loop(0, count, unroll=4)
    def _(k):
        r = rows[k]
        place = following[r]
        following[r] = place + 1
        span = jnp.int32(0)
        for s in range(1, spans):
            span = span + (cols[k] >= s * row_tiles).astype(jnp.int32)
        even = jnp.where(span >= 2, span - 2, span + 3)
        other = jnp.where(span <= 2, 2 - span, 7 - span)
        buf = jnp.where(swapped, other, even)
        flat = buf * row_tiles + cols[k] - span * row_tiles

        @pl.when(r < row_tiles)
        def _():
            pairs[place] = k + 128 * flat
            heads[place >> 1] = r

    helps, share, lanes = extra.shape
    mine = cot_v.shape[1] // helps
    high = bias[...].astype(jnp.bfloat16)
    rest = bias[...] - high.astype(jnp.float32)
    middle = rest.astype(jnp.bfloat16)
    low = (rest - middle.astype(jnp.float32)).astype(jnp.bfloat16)
    lane = lax.broadcasted_iota(jnp.int32, (share, lanes - mine), 1)
    bias_parts = jnp.where(lane == 0, high, jnp.where(lane == 1, middle, low))
    for copy in copies:
        copy.wait()
    for h in range(helps):
        extra[h, :, :mine] = cot_v[:, h * mine : (h + 1) * mine]
        extra[h, :, mine:] = bias_parts


def middle_kernel(parts, weight_t, out):
    helps, length, width = out.shape
    share = width // helps
    mine = length - 2 * share
    total = parts[0, :mine].astype(jnp.float32)
    for s in range(1, helps):
        total = total + parts[s, :mine].astype(jnp.float32)
    agg = total.astype(jnp.bfloat16)
    cotb = jnp.concatenate([parts[s, mine:] for s in range(helps)], axis=0)
    extra = cotb[:, mine:].astype(jnp.float32)
    bias = extra[:, 0:1] + extra[:, 1:2] + extra[:, 2:3]
    pre = lax.dot_general(weight_t[...], agg, NT, preferred_element_type=jnp.float32) + bias
    decay = jnp.exp(jnp.minimum(pre, 0.0))
    slope = jnp.where(pre > 0.0, 1.0, decay)
    grad = (cotb[:, :mine].astype(jnp.float32) * slope).astype(jnp.bfloat16)
    back = lax.dot_general(
        grad, weight_t[...], TN, preferred_element_type=jnp.float32
    ).astype(jnp.bfloat16)
    terms = lax.dot_general(grad, agg, NN, preferred_element_type=jnp.float32).astype(jnp.bfloat16)
    result = jnp.where(pre > 0.0, pre, decay - 1.0).astype(jnp.bfloat16)
    sums = jnp.sum(grad.astype(jnp.float32), axis=1, keepdims=True)
    high = sums.astype(jnp.bfloat16)
    low = (sums - high.astype(jnp.float32)).astype(jnp.bfloat16)
    lane = lax.broadcasted_iota(jnp.int32, (width, width - mine), 1)
    sums = jnp.where(lane == 0, high, low)
    for h in range(helps):
        own = slice(h * share, (h + 1) * share)
        out[h, :mine, :] = back
        out[h, mine : mine + share, :] = terms[own]
        out[h, mine + share :, :mine] = result[own]
        out[h, mine + share :, mine:] = sums[own]


def divide_kernel(parts, back, out, total, side, sums_v, sems):
    helps, _, width = parts.shape
    mine = back.shape[0] // helps
    share = total.shape[1]
    copies = []
    for s in range(helps):
        copies.append(pltpu.make_async_copy(parts.at[s, mine:], side.at[s], sems.at[s]))
        copies.append(
            pltpu.make_async_copy(
                parts.at[s, :mine], back.at[s * mine : (s + 1) * mine], sems.at[helps + s]
            )
        )
    for copy in copies:
        copy.start()
    for copy in copies[0::2]:
        copy.wait()
    sums = side[0].astype(jnp.float32)
    for s in range(1, helps):
        sums = sums + side[s].astype(jnp.float32)
    both = sums[share:, mine : mine + 1] + sums[share:, mine + 1 : mine + 2]
    both = jnp.broadcast_to(both, (share, total.shape[2] - width))
    sums_v[:, :width] = sums[:share]
    sums_v[:, width:] = both
    copies = copies[1::2]
    for s in range(total.shape[0]):
        copies.append(pltpu.make_async_copy(sums_v, total.at[s], sems.at[2 * helps + s]))
        copies[helps + s].start()
    for s in range(helps):
        out[:, s * mine : (s + 1) * mine] = side[s, share:, :mine]
    for copy in copies:
        copy.wait()


def spread(x):
    return lax.all_to_all(x, "help", 0, 0)


def round_of_four(total, one, two):
    got = [
        move(total, functools.partial(lambda s, b, h: (b ^ s, h), s)) for s in (one, two, one ^ two)
    ]
    return (total + got[0]) + (got[1] + got[2])


def fours(blks, one, two):
    bases = [b for b in range(blks) if b & (one | two) == 0]
    return [[b, b | one, b | two, b | one | two] for b in bases]


def per_device(features_t, weight, bias, cotangent_t, tile_vals, slot_row, slot_col):
    tiles = tile_vals[0, 0]
    tile = tiles.shape[-1]
    width, nodes = features_t.shape
    row_tiles = nodes // tile
    helps = lax.axis_size("help")
    blks = lax.axis_size("blk")
    share = cotangent_t.shape[0]
    mine = nodes // helps
    count = tiles.shape[0]
    swap = lambda b, h: (b ^ 1, h)

    zero, one, two = near(features_t)
    pair_count = (count + row_tiles + 3) // 4 * 2
    pairs, heads, extra, weight_t, tiles, own = pl.pallas_call(
        functools.partial(prepare_kernel, row_tiles),
        out_shape=(
            jax.ShapeDtypeStruct((2 * pair_count,), jnp.int32),
            jax.ShapeDtypeStruct((pair_count,), jnp.int32),
            jax.ShapeDtypeStruct((helps, share, width), jnp.bfloat16),
            jax.ShapeDtypeStruct(weight.shape, jnp.bfloat16),
            pltpu.VMEM(tiles.shape, jnp.bfloat16),
            pltpu.VMEM(features_t.shape, jnp.bfloat16),
        ),
        in_specs=[SMEM] * 3 + [VMEM] * 2 + [ANY] * 3,
        out_specs=(SMEM,) * 2 + (VMEM,) * 2 + (ANY,) * 2,
        scratch_shapes=[
            pltpu.SMEM((row_tiles + 1,), jnp.int32),
            pltpu.VMEM(cotangent_t.shape, jnp.bfloat16),
            pltpu.SemaphoreType.DMA((3,)),
        ],
        compiler_params=pltpu.CompilerParams(vmem_limit_bytes=4 * 2**20),
    )(
        (lax.axis_index("blk") % 2).astype(jnp.int32).reshape(1),
        slot_row[0, 0],
        slot_col[0, 0],
        bias.reshape(share, 1),
        weight,
        *(pltpu.with_memory_space_constraint(x, pltpu.HBM) for x in (tiles, cotangent_t, features_t)),
    )
    slots = (pairs, heads)
    three = move(after(one, own), swap)
    sent = aggregate(
        forward_kernel,
        (own, zero, one, two, three),
        tiles,
        slots,
        (helps, mine + share, width),
        extra,
    )
    length = mine + 2 * share
    sent = pl.pallas_call(
        middle_kernel,
        out_shape=jax.ShapeDtypeStruct((helps, length, width), jnp.bfloat16),
        in_specs=[VMEM] * 2,
        out_specs=VMEM,
        compiler_params=pltpu.CompilerParams(vmem_limit_bytes=16 * 2**20),
    )(spread(sent), weight_t)
    back, output, total = pl.pallas_call(
        divide_kernel,
        out_shape=(
            pltpu.VMEM((nodes, width), jnp.bfloat16),
            jax.ShapeDtypeStruct((share, nodes), jnp.bfloat16),
            pltpu.HBM((4, share, width + tile), jnp.float32),
        ),
        in_specs=[ANY],
        out_specs=(ANY, VMEM, ANY),
        scratch_shapes=[
            pltpu.VMEM((helps, 2 * share, width), jnp.bfloat16),
            pltpu.VMEM((share, width + tile), jnp.float32),
            pltpu.SemaphoreType.DMA((2 * helps + 4,)),
        ],
        compiler_params=pltpu.CompilerParams(vmem_limit_bytes=4 * 2**20),
    )(spread(sent))
    zero, one, two = near(back)
    half = blks // 2
    far = lax.all_to_all(total, "blk", 0, 0, axis_index_groups=fours(blks, 8, 16))
    total = jnp.sum(far, axis=0)
    three = move(after(one, (total, two)), swap)
    value = aggregate(
        backward_kernel, (back, zero, one, two, three), tiles, slots, (helps, share, nodes)
    )
    propagated = jnp.sum(spread(value).astype(jnp.float32), axis=0)
    total = round_of_four(total, 1, half)
    total = round_of_four(total, 2, 4)
    total = total * (1.0 / math.sqrt(nodes * blks))
    return (output, propagated, total[:, :width].T, total[:, width])


def solution(mesh):
    placed = (
        P(None, "blk"),
        P(),
        P("help"),
        P("help", "blk"),
        P("blk", "help", None, None, None),
        P("blk", "help", None),
        P("blk", "help", None),
    )
    return jax.shard_map(
        per_device,
        mesh=mesh,
        in_specs=placed,
        out_specs=(P("help", "blk"), P("help", "blk"), P(None, "help"), P("help")),
        check_vma=False,
    )
```

```python
import functools
import math

import jax
import jax.numpy as jnp
from jax import lax
from jax.experimental import pallas as pl
from jax.experimental.pallas import tpu as pltpu
from jax.sharding import PartitionSpec as P

BAND = 2
AXES = ("blk", "help")
ANY = pl.BlockSpec(memory_space=pl.ANY)
VMEM = pl.BlockSpec(memory_space=pltpu.VMEM)
SMEM = pl.BlockSpec(memory_space=pltpu.SMEM)
NT = (((1,), (1,)), ((), ()))
NN = (((1,), (0,)), ((), ()))
TN = (((0,), (0,)), ((), ()))


def move(block, source):
    blks, helps = lax.axis_size("blk"), lax.axis_size("help")
    route = []
    for b in range(blks):
        for h in range(helps):
            sb, sh = source(b, h)
            route.append(((sb % blks) * helps + sh, b * helps + h))
    return lax.ppermute(block, AXES, route)


def step_two(b, h, sign, blks):
    other = (b + 2 * sign) % blks
    half = blks // 2
    return (other, h if other // half == b // half else h ^ 1)


def after(value, other):
    return lax.optimization_barrier((value, other))[0]


def near(block):
    blks = lax.axis_size("blk")
    one = move(block, lambda b, h: step_two(b, h, 1 if b % 2 == 0 else -1, blks))
    zero = move(block, lambda b, h: (b ^ 1, h))
    two = move(block, lambda b, h: step_two(b, h, -1 if b % 2 == 0 else 1, blks))
    return zero, one, two


def unit(size):
    place = (size, size)
    return (
        lax.broadcasted_iota(jnp.int32, place, 0) == lax.broadcasted_iota(jnp.int32, place, 1)
    ).astype(jnp.bfloat16)


def load_all(refs, places, sems):
    copies = [
        pltpu.make_async_copy(ref, place, sems.at[i])
        for i, (ref, place) in enumerate(zip(refs, places))
    ]
    for copy in copies:
        copy.start()
    return copies


def add_pairs(pairs, rows, tiles, acc, piece, axis, dims):
    tile = tiles.shape[1]
    count = rows.shape[0]
    unroll = count // 2

    @pl.loop(0, count // unroll)
    def _(step):
        for j in range(unroll):
            i = step * unroll + j
            one, two = pairs[2 * i], pairs[2 * i + 1]
            left = jnp.concatenate([tiles[one & 127], tiles[two & 127]], axis=1)
            right = jnp.concatenate(
                [piece(pl.multiple_of((s >> 7) * tile, tile)) for s in (one, two)], axis=axis
            )
            product = lax.dot_general(left, right, dims, preferred_element_type=jnp.float32)
            acc[pl.ds(pl.multiple_of(rows[i] * tile, tile), tile), :] += product


def forward_kernel(pairs, rows, b0, b1, b2, b3, b4, tiles, extra, out, win, acc, sems, stage, out_sems):
    tile = tiles.shape[1]
    nodes = b0.shape[1]
    helps = out.shape[0]
    mine = nodes // helps
    refs = (b0, b1, b2, b3, b4)
    copies = load_all(refs, [win.at[:, i * nodes : (i + 1) * nodes] for i in range(5)], sems)
    leaving = []
    for h in range(helps):
        leaving.append(pltpu.make_async_copy(extra.at[h], out.at[h, mine:], out_sems.at[helps + h]))
        leaving[h].start()
    acc[...] = jnp.zeros_like(acc)
    win[:, 5 * nodes :] = jnp.zeros((win.shape[0], tile), jnp.bfloat16)
    for copy in copies:
        copy.wait()
    add_pairs(pairs, rows, tiles, acc, lambda c: win[:, pl.ds(c, tile)], 1, NT)
    for h in range(helps):
        stage[h] = acc[h * mine : (h + 1) * mine, :].astype(jnp.bfloat16)
        leaving.append(pltpu.make_async_copy(stage.at[h], out.at[h, :mine], out_sems.at[h]))
        leaving[helps + h].start()
    for copy in leaving:
        copy.wait()


def backward_kernel(pairs, rows, b0, b1, b2, b3, b4, tiles, out, win, acc, sems, stage, out_sems):
    tile = tiles.shape[1]
    helps, share, nodes = out.shape
    width = helps * share
    refs = (b0, b1, b2, b3, b4)
    copies = load_all(refs, [win.at[i * nodes : (i + 1) * nodes, :] for i in range(5)], sems)
    acc[...] = jnp.zeros_like(acc)
    win[5 * nodes :, :] = jnp.zeros((tile, win.shape[1]), jnp.bfloat16)
    for copy in copies:
        copy.wait()
    add_pairs(pairs, rows, tiles, acc, lambda c: win[pl.ds(c, tile), :], 0, NN)
    eye = unit(width)
    for t in range(nodes // tile):
        part = acc[t * tile : (t + 1) * tile, :].astype(jnp.bfloat16)
        turned = lax.dot_general(eye, part, NT, preferred_element_type=jnp.float32)
        stage[:, :, t * tile : (t + 1) * tile] = turned.astype(jnp.bfloat16).reshape(helps, share, tile)
    leaving = [pltpu.make_async_copy(stage.at[h], out.at[h], out_sems.at[h]) for h in range(helps)]
    for copy in leaving:
        copy.start()
    for copy in leaving:
        copy.wait()


def aggregate(kernel, blocks, tiles, slots, out_shape, *extra):
    count, tile = tiles.shape[0], tiles.shape[1]
    nodes = max(blocks[0].shape)
    width = min(blocks[0].shape)
    forward = blocks[0].shape[1] == nodes
    span = 5 * nodes + tile
    parts = out_shape[0]
    return pl.pallas_call(
        kernel,
        out_shape=pltpu.HBM(out_shape, jnp.bfloat16),
        in_specs=[SMEM] * 2 + [ANY] * 5 + [VMEM] + [ANY] * len(extra),
        out_specs=ANY,
        scratch_shapes=[
            pltpu.VMEM((width, span) if forward else (span, width), jnp.bfloat16),
            pltpu.VMEM((nodes + tile, width), jnp.float32),
            pltpu.SemaphoreType.DMA((5,)),
            pltpu.VMEM((parts, nodes // parts, width) if forward else out_shape, jnp.bfloat16),
            pltpu.SemaphoreType.DMA((2 * parts,)),
        ],
        compiler_params=pltpu.CompilerParams(vmem_limit_bytes=20 * 2**20),
        cost_estimate=pl.CostEstimate(
            flops=2 * count * tile * tile * width,
            bytes_accessed=6 * 2**20,
            transcendentals=0,
        ),
    )(*slots, *blocks, tiles, *extra)


def prepare_kernel(row_tiles, odd, rows, cols, bias, weight, tiles, cot, own, pairs, heads, extra, weight_t, tiles_v, own_v, following, cot_v, sems):
    copies = load_all((tiles, cot, own), (tiles_v, cot_v, own_v), sems)
    weight_t[...] = lax.dot_general(
        unit(weight.shape[0]), weight[...], NT, preferred_element_type=jnp.float32
    ).astype(jnp.bfloat16)
    spans = 2 * BAND + 1
    count = rows.shape[0]
    for r in range(row_tiles + 1):
        following[r] = 0

    @pl.loop(0, count, unroll=4)
    def _(k):
        r = rows[k]
        following[r] = following[r] + 1

    first = jnp.int32(0)
    for r in range(row_tiles):
        used = following[r]
        following[r] = first
        first = first + ((used + 1) >> 1) * 2
    following[row_tiles] = jnp.int32(pairs.shape[0])

    @pl.loop(0, heads.shape[0], unroll=4)
    def _(i):
        heads[i] = row_tiles
        pairs[2 * i] = 128 * spans * row_tiles
        pairs[2 * i + 1] = 128 * spans * row_tiles

    swapped = odd[0] == 1

    @pl.loop(0, count, unroll=4)
    def _(k):
        r = rows[k]
        place = following[r]
        following[r] = place + 1
        span = jnp.int32(0)
        for s in range(1, spans):
            span = span + (cols[k] >= s * row_tiles).astype(jnp.int32)
        even = jnp.where(span >= 2, span - 2, span + 3)
        other = jnp.where(span <= 2, 2 - span, 7 - span)
        buf = jnp.where(swapped, other, even)
        flat = buf * row_tiles + cols[k] - span * row_tiles

        @pl.when(r < row_tiles)
        def _():
            pairs[place] = k + 128 * flat
            heads[place >> 1] = r

    helps, share, lanes = extra.shape
    mine = cot_v.shape[1] // helps
    high = bias[...].astype(jnp.bfloat16)
    rest = bias[...] - high.astype(jnp.float32)
    middle = rest.astype(jnp.bfloat16)
    low = (rest - middle.astype(jnp.float32)).astype(jnp.bfloat16)
    lane = lax.broadcasted_iota(jnp.int32, (share, lanes - mine), 1)
    bias_parts = jnp.where(lane == 0, high, jnp.where(lane == 1, middle, low))
    for copy in copies:
        copy.wait()
    for h in range(helps):
        extra[h, :, :mine] = cot_v[:, h * mine : (h + 1) * mine]
        extra[h, :, mine:] = bias_parts


def middle_kernel(parts, weight_t, back, side):
    helps, length, width = side.shape
    share = width // helps
    mine = back.shape[0]
    total = parts[0, :mine].astype(jnp.float32)
    for s in range(1, helps):
        total = total + parts[s, :mine].astype(jnp.float32)
    agg = total.astype(jnp.bfloat16)
    cotb = jnp.concatenate([parts[s, mine:] for s in range(helps)], axis=0)
    extra = cotb[:, mine:].astype(jnp.float32)
    bias = extra[:, 0:1] + extra[:, 1:2] + extra[:, 2:3]
    pre = lax.dot_general(weight_t[...], agg, NT, preferred_element_type=jnp.float32) + bias
    decay = jnp.exp(jnp.minimum(pre, 0.0))
    slope = jnp.where(pre > 0.0, 1.0, decay)
    grad = (cotb[:, :mine].astype(jnp.float32) * slope).astype(jnp.bfloat16)
    back[...] = lax.dot_general(
        grad, weight_t[...], TN, preferred_element_type=jnp.float32
    ).astype(jnp.bfloat16)
    terms = lax.dot_general(grad, agg, NN, preferred_element_type=jnp.float32).astype(jnp.bfloat16)
    result = jnp.where(pre > 0.0, pre, decay - 1.0).astype(jnp.bfloat16)
    sums = jnp.sum(grad.astype(jnp.float32), axis=1, keepdims=True)
    high = sums.astype(jnp.bfloat16)
    low = (sums - high.astype(jnp.float32)).astype(jnp.bfloat16)
    lane = lax.broadcasted_iota(jnp.int32, (width, width - mine), 1)
    sums = jnp.where(lane == 0, high, low)
    for h in range(helps):
        own = slice(h * share, (h + 1) * share)
        side[h, :share, :] = terms[own]
        side[h, share:, :mine] = result[own]
        side[h, share:, mine:] = sums[own]


def divide_kernel(side, out, total):
    helps, length, width = side.shape
    share = length // 2
    mine = out.shape[1] // helps
    sums = side[0].astype(jnp.float32)
    for s in range(1, helps):
        sums = sums + side[s].astype(jnp.float32)
    both = sums[share:, mine : mine + 1] + sums[share:, mine + 1 : mine + 2]
    both = jnp.broadcast_to(both, (share, width))
    for i in range(share):
        total[i] = sums[i : i + 1, :]
        total[share + i] = both[i : i + 1, :]
    for s in range(helps):
        out[:, s * mine : (s + 1) * mine] = side[s, share:, :mine]


def gather_row_kernel(rows, out):
    row = rows[0]
    for i in range(1, rows.shape[0]):
        row = row + rows[i]
    for i in range(out.shape[0]):
        out[i] = row


def place_kernel(turn, *refs):
    *parts, out, sems = refs
    count = len(parts)
    copies = []
    for i, part in enumerate(parts):
        at = lax.rem(turn[0] + i, count)
        copies.append(pltpu.make_async_copy(part, out.at[at], sems.at[i]))
        copies[i].start()
    for copy in copies:
        copy.wait()


def in_place(space, turn, *parts):
    return pl.pallas_call(
        place_kernel,
        out_shape=space((len(parts),) + parts[0].shape, parts[0].dtype),
        in_specs=[SMEM] + [ANY] * len(parts),
        out_specs=ANY,
        scratch_shapes=[pltpu.SemaphoreType.DMA((len(parts),))],
        compiler_params=pltpu.CompilerParams(vmem_limit_bytes=2 * 2**20),
    )(turn.reshape(1), *(pltpu.with_memory_space_constraint(x, pltpu.HBM) for x in parts))


def spread(x):
    return lax.all_to_all(x, "help", 0, 0)


def per_device(features_t, weight, bias, cotangent_t, tile_vals, slot_row, slot_col):
    tiles = tile_vals[0, 0]
    tile = tiles.shape[-1]
    width, nodes = features_t.shape
    row_tiles = nodes // tile
    helps = lax.axis_size("help")
    blks = lax.axis_size("blk")
    share = cotangent_t.shape[0]
    mine = nodes // helps
    count = tiles.shape[0]
    swap = lambda b, h: (b ^ 1, h)

    zero, one, two = near(features_t)
    pair_count = (count + row_tiles + 3) // 4 * 2
    pairs, heads, extra, weight_t, tiles, own = pl.pallas_call(
        functools.partial(prepare_kernel, row_tiles),
        out_shape=(
            jax.ShapeDtypeStruct((2 * pair_count,), jnp.int32),
            jax.ShapeDtypeStruct((pair_count,), jnp.int32),
            jax.ShapeDtypeStruct((helps, share, width), jnp.bfloat16),
            jax.ShapeDtypeStruct(weight.shape, jnp.bfloat16),
            pltpu.VMEM(tiles.shape, jnp.bfloat16),
            pltpu.VMEM(features_t.shape, jnp.bfloat16),
        ),
        in_specs=[SMEM] * 3 + [VMEM] * 2 + [ANY] * 3,
        out_specs=(SMEM,) * 2 + (VMEM,) * 2 + (ANY,) * 2,
        scratch_shapes=[
            pltpu.SMEM((row_tiles + 1,), jnp.int32),
            pltpu.VMEM(cotangent_t.shape, jnp.bfloat16),
            pltpu.SemaphoreType.DMA((3,)),
        ],
        compiler_params=pltpu.CompilerParams(vmem_limit_bytes=4 * 2**20),
    )(
        (lax.axis_index("blk") % 2).astype(jnp.int32).reshape(1),
        slot_row[0, 0],
        slot_col[0, 0],
        bias.reshape(share, 1),
        weight,
        *(pltpu.with_memory_space_constraint(x, pltpu.HBM) for x in (tiles, cotangent_t, features_t)),
    )
    slots = (pairs, heads)
    three = move(after(one, own), swap)
    sent = aggregate(
        forward_kernel,
        (own, zero, one, two, three),
        tiles,
        slots,
        (helps, mine + share, width),
        extra,
    )
    back, side = pl.pallas_call(
        middle_kernel,
        out_shape=(
            jax.ShapeDtypeStruct((mine, width), jnp.bfloat16),
            jax.ShapeDtypeStruct((helps, 2 * share, width), jnp.bfloat16),
        ),
        in_specs=[VMEM] * 2,
        out_specs=(VMEM,) * 2,
        compiler_params=pltpu.CompilerParams(vmem_limit_bytes=16 * 2**20),
    )(spread(sent), weight_t)
    helper = lax.axis_index("help").astype(jnp.int32)
    pair = in_place(pltpu.HBM, helper & 1, back, move(back, lambda b, h: (b, h ^ 1)))
    along = lambda d: functools.partial(lambda d, b, h: (b, (h + 2 * d) % helps), d)
    back = in_place(pltpu.VMEM, helper >> 1, pair, *(move(pair, along(d)) for d in range(1, helps // 2)))
    back = back.reshape(nodes, width)

    output, total = pl.pallas_call(
        divide_kernel,
        out_shape=(
            jax.ShapeDtypeStruct((share, nodes), jnp.bfloat16),
            jax.ShapeDtypeStruct((blks, 1, width), jnp.float32),
        ),
        in_specs=[VMEM],
        out_specs=(VMEM, VMEM),
        compiler_params=pltpu.CompilerParams(vmem_limit_bytes=4 * 2**20),
    )(spread(side))
    back = after(back, total)
    total = pl.pallas_call(
        gather_row_kernel,
        out_shape=jax.ShapeDtypeStruct(total.shape, jnp.float32),
        in_specs=[VMEM],
        out_specs=VMEM,
        compiler_params=pltpu.CompilerParams(vmem_limit_bytes=2 * 2**20),
    )(lax.all_to_all(total, "blk", 0, 0))
    zero, one, two = near(back)
    three = move(after(one, (total, two)), swap)
    total = lax.all_to_all(total, "blk", 0, 0)
    value = aggregate(
        backward_kernel, (back, zero, one, two, three), tiles, slots, (helps, share, nodes)
    )
    propagated = jnp.sum(spread(after(value, total)).astype(jnp.float32), axis=0)
    total = total[:, 0, :] * (1.0 / math.sqrt(nodes * blks))
    return (output, propagated, total[:share].T, total[share:, 0])


def solution(mesh):
    placed = (
        P(None, "blk"),
        P(),
        P("help"),
        P("help", "blk"),
        P("blk", "help", None, None, None),
        P("blk", "help", None),
        P("blk", "help", None),
    )
    return jax.shard_map(
        per_device,
        mesh=mesh,
        in_specs=placed,
        out_specs=(P("help", "blk"), P("help", "blk"), P(None, "help"), P("help")),
        check_vma=False,
    )
```

```python
import functools
import math

import jax
import jax.numpy as jnp
from jax import lax
from jax.experimental import pallas as pl
from jax.experimental.pallas import tpu as pltpu
from jax.sharding import PartitionSpec as P

BAND = 2
AXES = ("blk", "help")
ANY = pl.BlockSpec(memory_space=pl.ANY)
VMEM = pl.BlockSpec(memory_space=pltpu.VMEM)
SMEM = pl.BlockSpec(memory_space=pltpu.SMEM)
NT = (((1,), (1,)), ((), ()))
NN = (((1,), (0,)), ((), ()))
TN = (((0,), (0,)), ((), ()))


def move(block, source):
    blks, helps = lax.axis_size("blk"), lax.axis_size("help")
    route = []
    for b in range(blks):
        for h in range(helps):
            sb, sh = source(b, h)
            route.append(((sb % blks) * helps + sh, b * helps + h))
    return lax.ppermute(block, AXES, route)


def step_two(b, h, sign, blks):
    other = (b + 2 * sign) % blks
    half = blks // 2
    return (other, h if other // half == b // half else h ^ 1)


def after(value, other):
    return lax.optimization_barrier((value, other))[0]


def near(block):
    blks = lax.axis_size("blk")
    one = move(block, lambda b, h: step_two(b, h, 1 if b % 2 == 0 else -1, blks))
    zero = move(block, lambda b, h: (b ^ 1, h))
    two = move(block, lambda b, h: step_two(b, h, -1 if b % 2 == 0 else 1, blks))
    return zero, one, two


def unit(size):
    place = (size, size)
    return (
        lax.broadcasted_iota(jnp.int32, place, 0) == lax.broadcasted_iota(jnp.int32, place, 1)
    ).astype(jnp.bfloat16)


def load_all(refs, places, sems):
    copies = [
        pltpu.make_async_copy(ref, place, sems.at[i])
        for i, (ref, place) in enumerate(zip(refs, places))
    ]
    for copy in copies:
        copy.start()
    return copies


def add_pairs(pairs, rows, tiles, acc, piece, axis, dims):
    tile = tiles.shape[1]
    count = rows.shape[0]
    unroll = count // 2

    @pl.loop(0, count // unroll)
    def _(step):
        for j in range(unroll):
            i = step * unroll + j
            one, two = pairs[2 * i], pairs[2 * i + 1]
            left = jnp.concatenate([tiles[one & 127], tiles[two & 127]], axis=1)
            right = jnp.concatenate(
                [piece(pl.multiple_of((s >> 7) * tile, tile)) for s in (one, two)], axis=axis
            )
            product = lax.dot_general(left, right, dims, preferred_element_type=jnp.float32)
            acc[pl.ds(pl.multiple_of(rows[i] * tile, tile), tile), :] += product


def forward_kernel(pairs, rows, b0, b1, b2, b3, b4, tiles, extra, out, win, acc, sems, stage, out_sems):
    tile = tiles.shape[1]
    nodes = b0.shape[1]
    helps = out.shape[0]
    mine = nodes // helps
    refs = (b0, b1, b2, b3, b4)
    copies = load_all(refs, [win.at[:, i * nodes : (i + 1) * nodes] for i in range(5)], sems)
    leaving = []
    for h in range(helps):
        leaving.append(pltpu.make_async_copy(extra.at[h], out.at[h, mine:], out_sems.at[helps + h]))
        leaving[h].start()
    acc[...] = jnp.zeros_like(acc)
    win[:, 5 * nodes :] = jnp.zeros((win.shape[0], tile), jnp.bfloat16)
    for copy in copies:
        copy.wait()
    add_pairs(pairs, rows, tiles, acc, lambda c: win[:, pl.ds(c, tile)], 1, NT)
    for h in range(helps):
        stage[h] = acc[h * mine : (h + 1) * mine, :].astype(jnp.bfloat16)
        leaving.append(pltpu.make_async_copy(stage.at[h], out.at[h, :mine], out_sems.at[h]))
        leaving[helps + h].start()
    for copy in leaving:
        copy.wait()


def backward_kernel(pairs, rows, b0, b1, b2, b3, b4, tiles, out, win, acc, sems, stage, out_sems):
    tile = tiles.shape[1]
    helps, share, nodes = out.shape
    width = helps * share
    refs = (b0, b1, b2, b3, b4)
    copies = load_all(refs, [win.at[i * nodes : (i + 1) * nodes, :] for i in range(5)], sems)
    acc[...] = jnp.zeros_like(acc)
    win[5 * nodes :, :] = jnp.zeros((tile, win.shape[1]), jnp.bfloat16)
    for copy in copies:
        copy.wait()
    add_pairs(pairs, rows, tiles, acc, lambda c: win[pl.ds(c, tile), :], 0, NN)
    eye = unit(width)
    for t in range(nodes // tile):
        part = acc[t * tile : (t + 1) * tile, :].astype(jnp.bfloat16)
        turned = lax.dot_general(eye, part, NT, preferred_element_type=jnp.float32)
        stage[:, :, t * tile : (t + 1) * tile] = turned.astype(jnp.bfloat16).reshape(helps, share, tile)
    leaving = [pltpu.make_async_copy(stage.at[h], out.at[h], out_sems.at[h]) for h in range(helps)]
    for copy in leaving:
        copy.start()
    for copy in leaving:
        copy.wait()


def aggregate(kernel, blocks, tiles, slots, out_shape, *extra):
    count, tile = tiles.shape[0], tiles.shape[1]
    nodes = max(blocks[0].shape)
    width = min(blocks[0].shape)
    forward = blocks[0].shape[1] == nodes
    span = 5 * nodes + tile
    parts = out_shape[0]
    return pl.pallas_call(
        kernel,
        out_shape=pltpu.HBM(out_shape, jnp.bfloat16),
        in_specs=[SMEM] * 2 + [ANY] * 5 + [VMEM] + [ANY] * len(extra),
        out_specs=ANY,
        scratch_shapes=[
            pltpu.VMEM((width, span) if forward else (span, width), jnp.bfloat16),
            pltpu.VMEM((nodes + tile, width), jnp.float32),
            pltpu.SemaphoreType.DMA((5,)),
            pltpu.VMEM((parts, nodes // parts, width) if forward else out_shape, jnp.bfloat16),
            pltpu.SemaphoreType.DMA((2 * parts,)),
        ],
        compiler_params=pltpu.CompilerParams(vmem_limit_bytes=20 * 2**20),
        cost_estimate=pl.CostEstimate(
            flops=2 * count * tile * tile * width,
            bytes_accessed=6 * 2**20,
            transcendentals=0,
        ),
    )(*slots, *blocks, tiles, *extra)


def prepare_kernel(row_tiles, odd, rows, cols, bias, weight, tiles, cot, own, pairs, heads, extra, weight_t, tiles_v, own_v, following, cot_v, sems):
    copies = load_all((tiles, cot, own), (tiles_v, cot_v, own_v), sems)
    weight_t[...] = lax.dot_general(
        unit(weight.shape[0]), weight[...], NT, preferred_element_type=jnp.float32
    ).astype(jnp.bfloat16)
    spans = 2 * BAND + 1
    count = rows.shape[0]
    for r in range(row_tiles + 1):
        following[r] = 0

    @pl.loop(0, count, unroll=4)
    def _(k):
        r = rows[k]
        following[r] = following[r] + 1

    first = jnp.int32(0)
    for r in range(row_tiles):
        used = following[r]
        following[r] = first
        first = first + ((used + 1) >> 1) * 2
    following[row_tiles] = jnp.int32(pairs.shape[0])

    @pl.loop(0, heads.shape[0], unroll=4)
    def _(i):
        heads[i] = row_tiles
        pairs[2 * i] = 128 * spans * row_tiles
        pairs[2 * i + 1] = 128 * spans * row_tiles

    swapped = odd[0] == 1

    @pl.loop(0, count, unroll=4)
    def _(k):
        r = rows[k]
        place = following[r]
        following[r] = place + 1
        span = jnp.int32(0)
        for s in range(1, spans):
            span = span + (cols[k] >= s * row_tiles).astype(jnp.int32)
        even = jnp.where(span >= 2, span - 2, span + 3)
        other = jnp.where(span <= 2, 2 - span, 7 - span)
        buf = jnp.where(swapped, other, even)
        flat = buf * row_tiles + cols[k] - span * row_tiles

        @pl.when(r < row_tiles)
        def _():
            pairs[place] = k + 128 * flat
            heads[place >> 1] = r

    helps, share, lanes = extra.shape
    mine = cot_v.shape[1] // helps
    high = bias[...].astype(jnp.bfloat16)
    rest = bias[...] - high.astype(jnp.float32)
    middle = rest.astype(jnp.bfloat16)
    low = (rest - middle.astype(jnp.float32)).astype(jnp.bfloat16)
    lane = lax.broadcasted_iota(jnp.int32, (share, lanes - mine), 1)
    bias_parts = jnp.where(lane == 0, high, jnp.where(lane == 1, middle, low))
    for copy in copies:
        copy.wait()
    for h in range(helps):
        extra[h, :, :mine] = cot_v[:, h * mine : (h + 1) * mine]
        extra[h, :, mine:] = bias_parts


def middle_kernel(parts, weight_t, out):
    helps, length, width = out.shape
    share = width // helps
    mine = length - 2 * share
    total = parts[0, :mine].astype(jnp.float32)
    for s in range(1, helps):
        total = total + parts[s, :mine].astype(jnp.float32)
    agg = total.astype(jnp.bfloat16)
    cotb = jnp.concatenate([parts[s, mine:] for s in range(helps)], axis=0)
    extra = cotb[:, mine:].astype(jnp.float32)
    bias = extra[:, 0:1] + extra[:, 1:2] + extra[:, 2:3]
    pre = lax.dot_general(weight_t[...], agg, NT, preferred_element_type=jnp.float32) + bias
    decay = jnp.exp(jnp.minimum(pre, 0.0))
    slope = jnp.where(pre > 0.0, 1.0, decay)
    grad = (cotb[:, :mine].astype(jnp.float32) * slope).astype(jnp.bfloat16)
    back = lax.dot_general(
        grad, weight_t[...], TN, preferred_element_type=jnp.float32
    ).astype(jnp.bfloat16)
    terms = lax.dot_general(grad, agg, NN, preferred_element_type=jnp.float32).astype(jnp.bfloat16)
    result = jnp.where(pre > 0.0, pre, decay - 1.0).astype(jnp.bfloat16)
    sums = jnp.sum(grad.astype(jnp.float32), axis=1, keepdims=True)
    high = sums.astype(jnp.bfloat16)
    low = (sums - high.astype(jnp.float32)).astype(jnp.bfloat16)
    lane = lax.broadcasted_iota(jnp.int32, (width, width - mine), 1)
    sums = jnp.where(lane == 0, high, low)
    for h in range(helps):
        own = slice(h * share, (h + 1) * share)
        out[h, :mine, :] = back
        out[h, mine : mine + share, :] = terms[own]
        out[h, mine + share :, :mine] = result[own]
        out[h, mine + share :, mine:] = sums[own]


def divide_kernel(parts, back, out, total, side, sums_v, sems):
    helps, _, width = parts.shape
    mine = back.shape[0] // helps
    share = total.shape[1]
    copies = []
    for s in range(helps):
        copies.append(pltpu.make_async_copy(parts.at[s, mine:], side.at[s], sems.at[s]))
        copies.append(
            pltpu.make_async_copy(
                parts.at[s, :mine], back.at[s * mine : (s + 1) * mine], sems.at[helps + s]
            )
        )
    for copy in copies:
        copy.start()
    for copy in copies[0::2]:
        copy.wait()
    sums = side[0].astype(jnp.float32)
    for s in range(1, helps):
        sums = sums + side[s].astype(jnp.float32)
    both = sums[share:, mine : mine + 1] + sums[share:, mine + 1 : mine + 2]
    both = jnp.broadcast_to(both, (share, total.shape[2] - width))
    sums_v[:, :width] = sums[:share]
    sums_v[:, width:] = both
    copies = copies[1::2]
    for s in range(total.shape[0]):
        copies.append(pltpu.make_async_copy(sums_v, total.at[s], sems.at[2 * helps + s]))
        copies[helps + s].start()
    for s in range(helps):
        out[:, s * mine : (s + 1) * mine] = side[s, share:, :mine]
    for copy in copies:
        copy.wait()


def spread(x):
    return lax.all_to_all(x, "help", 0, 0)


def alike(blks, steps):
    return [[b for b in range(blks) if b & ~steps == base] for base in range(blks) if base & steps == 0]


def per_device(features_t, weight, bias, cotangent_t, tile_vals, slot_row, slot_col):
    tiles = tile_vals[0, 0]
    tile = tiles.shape[-1]
    width, nodes = features_t.shape
    row_tiles = nodes // tile
    helps = lax.axis_size("help")
    blks = lax.axis_size("blk")
    share = cotangent_t.shape[0]
    mine = nodes // helps
    count = tiles.shape[0]
    swap = lambda b, h: (b ^ 1, h)

    zero, one, two = near(features_t)
    pair_count = (count + row_tiles + 3) // 4 * 2
    pairs, heads, extra, weight_t, tiles, own = pl.pallas_call(
        functools.partial(prepare_kernel, row_tiles),
        out_shape=(
            jax.ShapeDtypeStruct((2 * pair_count,), jnp.int32),
            jax.ShapeDtypeStruct((pair_count,), jnp.int32),
            jax.ShapeDtypeStruct((helps, share, width), jnp.bfloat16),
            jax.ShapeDtypeStruct(weight.shape, jnp.bfloat16),
            pltpu.VMEM(tiles.shape, jnp.bfloat16),
            pltpu.VMEM(features_t.shape, jnp.bfloat16),
        ),
        in_specs=[SMEM] * 3 + [VMEM] * 2 + [ANY] * 3,
        out_specs=(SMEM,) * 2 + (VMEM,) * 2 + (ANY,) * 2,
        scratch_shapes=[
            pltpu.SMEM((row_tiles + 1,), jnp.int32),
            pltpu.VMEM(cotangent_t.shape, jnp.bfloat16),
            pltpu.SemaphoreType.DMA((3,)),
        ],
        compiler_params=pltpu.CompilerParams(vmem_limit_bytes=4 * 2**20),
    )(
        (lax.axis_index("blk") % 2).astype(jnp.int32).reshape(1),
        slot_row[0, 0],
        slot_col[0, 0],
        bias.reshape(share, 1),
        weight,
        *(pltpu.with_memory_space_constraint(x, pltpu.HBM) for x in (tiles, cotangent_t, features_t)),
    )
    slots = (pairs, heads)
    three = move(after(one, own), swap)
    sent = aggregate(
        forward_kernel,
        (own, zero, one, two, three),
        tiles,
        slots,
        (helps, mine + share, width),
        extra,
    )
    length = mine + 2 * share
    sent = pl.pallas_call(
        middle_kernel,
        out_shape=jax.ShapeDtypeStruct((helps, length, width), jnp.bfloat16),
        in_specs=[VMEM] * 2,
        out_specs=VMEM,
        compiler_params=pltpu.CompilerParams(vmem_limit_bytes=16 * 2**20),
    )(spread(sent), weight_t)
    back, output, total = pl.pallas_call(
        divide_kernel,
        out_shape=(
            pltpu.VMEM((nodes, width), jnp.bfloat16),
            jax.ShapeDtypeStruct((share, nodes), jnp.bfloat16),
            pltpu.HBM((8, share, width + tile), jnp.float32),
        ),
        in_specs=[ANY],
        out_specs=(ANY, VMEM, ANY),
        scratch_shapes=[
            pltpu.VMEM((helps, 2 * share, width), jnp.bfloat16),
            pltpu.VMEM((share, width + tile), jnp.float32),
            pltpu.SemaphoreType.DMA((2 * helps + 8,)),
        ],
        compiler_params=pltpu.CompilerParams(vmem_limit_bytes=4 * 2**20),
    )(spread(sent))
    zero, one, two = near(back)
    half = blks // 2
    far = lax.all_to_all(total, "blk", 0, 0, axis_index_groups=alike(blks, half | 3))
    total = jnp.sum(far, axis=0)
    three = move(after(one, (total, two)), swap)
    value = aggregate(
        backward_kernel, (back, zero, one, two, three), tiles, slots, (helps, share, nodes)
    )
    propagated = jnp.sum(spread(value).astype(jnp.float32), axis=0)
    for step in (16, 8, 4):
        total = total + move(total, functools.partial(lambda s, b, h: (b ^ s, h), step))
    total = total * (1.0 / math.sqrt(nodes * blks))
    return (output, propagated, total[:, :width].T, total[:, width])


def solution(mesh):
    placed = (
        P(None, "blk"),
        P(),
        P("help"),
        P("help", "blk"),
        P("blk", "help", None, None, None),
        P("blk", "help", None),
        P("blk", "help", None),
    )
    return jax.shard_map(
        per_device,
        mesh=mesh,
        in_specs=placed,
        out_specs=(P("help", "blk"), P("help", "blk"), P(None, "help"), P("help")),
        check_vma=False,
    )
```

```python
import functools
import math

import jax
import jax.numpy as jnp
from jax import lax
from jax.experimental import pallas as pl
from jax.experimental.pallas import tpu as pltpu
from jax.sharding import PartitionSpec as P

BAND = 2
AXES = ("blk", "help")
ANY = pl.BlockSpec(memory_space=pl.ANY)
VMEM = pl.BlockSpec(memory_space=pltpu.VMEM)
SMEM = pl.BlockSpec(memory_space=pltpu.SMEM)
NT = (((1,), (1,)), ((), ()))
NN = (((1,), (0,)), ((), ()))
TN = (((0,), (0,)), ((), ()))


def move(block, source):
    blks, helps = lax.axis_size("blk"), lax.axis_size("help")
    route = []
    for b in range(blks):
        for h in range(helps):
            sb, sh = source(b, h)
            route.append(((sb % blks) * helps + sh, b * helps + h))
    return lax.ppermute(block, AXES, route)


def step_two(b, h, sign, blks):
    other = (b + 2 * sign) % blks
    half = blks // 2
    return (other, h if other // half == b // half else h ^ 1)


def after(value, other):
    return lax.optimization_barrier((value, other))[0]


def near(block):
    blks = lax.axis_size("blk")
    one = move(block, lambda b, h: step_two(b, h, 1 if b % 2 == 0 else -1, blks))
    zero = move(block, lambda b, h: (b ^ 1, h))
    two = move(block, lambda b, h: step_two(b, h, -1 if b % 2 == 0 else 1, blks))
    return zero, one, two


def unit(size):
    place = (size, size)
    return (
        lax.broadcasted_iota(jnp.int32, place, 0) == lax.broadcasted_iota(jnp.int32, place, 1)
    ).astype(jnp.bfloat16)


def load_all(refs, places, sems):
    copies = [
        pltpu.make_async_copy(ref, place, sems.at[i])
        for i, (ref, place) in enumerate(zip(refs, places))
    ]
    for copy in copies:
        copy.start()
    return copies


def add_pairs(pairs, rows, tiles, acc, piece, axis, dims):
    tile = tiles.shape[1]
    count = rows.shape[0]
    unroll = count // 2

    @pl.loop(0, count // unroll)
    def _(step):
        for j in range(unroll):
            i = step * unroll + j
            one, two = pairs[2 * i], pairs[2 * i + 1]
            left = jnp.concatenate([tiles[one & 127], tiles[two & 127]], axis=1)
            right = jnp.concatenate(
                [piece(pl.multiple_of((s >> 7) * tile, tile)) for s in (one, two)], axis=axis
            )
            product = lax.dot_general(left, right, dims, preferred_element_type=jnp.float32)
            acc[pl.ds(pl.multiple_of(rows[i] * tile, tile), tile), :] += product


def forward_kernel(pairs, rows, b0, b1, b2, b3, b4, tiles, extra, out, win, acc, sems, stage, out_sems):
    tile = tiles.shape[1]
    nodes = b0.shape[1]
    helps = out.shape[0]
    mine = nodes // helps
    refs = (b0, b1, b2, b3, b4)
    copies = load_all(refs, [win.at[:, i * nodes : (i + 1) * nodes] for i in range(5)], sems)
    leaving = []
    for h in range(helps):
        leaving.append(pltpu.make_async_copy(extra.at[h], out.at[h, mine:], out_sems.at[helps + h]))
        leaving[h].start()
    acc[...] = jnp.zeros_like(acc)
    win[:, 5 * nodes :] = jnp.zeros((win.shape[0], tile), jnp.bfloat16)
    for copy in copies:
        copy.wait()
    add_pairs(pairs, rows, tiles, acc, lambda c: win[:, pl.ds(c, tile)], 1, NT)
    for h in range(helps):
        stage[h] = acc[h * mine : (h + 1) * mine, :].astype(jnp.bfloat16)
        leaving.append(pltpu.make_async_copy(stage.at[h], out.at[h, :mine], out_sems.at[h]))
        leaving[helps + h].start()
    for copy in leaving:
        copy.wait()


def backward_kernel(pairs, rows, b0, b1, b2, b3, b4, tiles, out, win, acc, sems, stage, out_sems):
    tile = tiles.shape[1]
    helps, share, nodes = out.shape
    width = helps * share
    refs = (b0, b1, b2, b3, b4)
    copies = load_all(refs, [win.at[i * nodes : (i + 1) * nodes, :] for i in range(5)], sems)
    acc[...] = jnp.zeros_like(acc)
    win[5 * nodes :, :] = jnp.zeros((tile, win.shape[1]), jnp.bfloat16)
    for copy in copies:
        copy.wait()
    add_pairs(pairs, rows, tiles, acc, lambda c: win[pl.ds(c, tile), :], 0, NN)
    eye = unit(width)
    for t in range(nodes // tile):
        part = acc[t * tile : (t + 1) * tile, :].astype(jnp.bfloat16)
        turned = lax.dot_general(eye, part, NT, preferred_element_type=jnp.float32)
        stage[:, :, t * tile : (t + 1) * tile] = turned.astype(jnp.bfloat16).reshape(helps, share, tile)
    leaving = [pltpu.make_async_copy(stage.at[h], out.at[h], out_sems.at[h]) for h in range(helps)]
    for copy in leaving:
        copy.start()
    for copy in leaving:
        copy.wait()


def aggregate(kernel, blocks, tiles, slots, out_shape, *extra):
    count, tile = tiles.shape[0], tiles.shape[1]
    nodes = max(blocks[0].shape)
    width = min(blocks[0].shape)
    forward = blocks[0].shape[1] == nodes
    span = 5 * nodes + tile
    parts = out_shape[0]
    return pl.pallas_call(
        kernel,
        out_shape=pltpu.HBM(out_shape, jnp.bfloat16),
        in_specs=[SMEM] * 2 + [ANY] * 5 + [VMEM] + [ANY] * len(extra),
        out_specs=ANY,
        scratch_shapes=[
            pltpu.VMEM((width, span) if forward else (span, width), jnp.bfloat16),
            pltpu.VMEM((nodes + tile, width), jnp.float32),
            pltpu.SemaphoreType.DMA((5,)),
            pltpu.VMEM((parts, nodes // parts, width) if forward else out_shape, jnp.bfloat16),
            pltpu.SemaphoreType.DMA((2 * parts,)),
        ],
        compiler_params=pltpu.CompilerParams(vmem_limit_bytes=20 * 2**20),
        cost_estimate=pl.CostEstimate(
            flops=2 * count * tile * tile * width,
            bytes_accessed=6 * 2**20,
            transcendentals=0,
        ),
    )(*slots, *blocks, tiles, *extra)


def prepare_kernel(row_tiles, odd, rows, cols, bias, weight, tiles, cot, own, pairs, heads, extra, weight_t, tiles_v, own_v, following, cot_v, sems):
    copies = load_all((tiles, cot, own), (tiles_v, cot_v, own_v), sems)
    weight_t[...] = lax.dot_general(
        unit(weight.shape[0]), weight[...], NT, preferred_element_type=jnp.float32
    ).astype(jnp.bfloat16)
    spans = 2 * BAND + 1
    count = rows.shape[0]
    for r in range(row_tiles + 1):
        following[r] = 0

    @pl.loop(0, count, unroll=4)
    def _(k):
        r = rows[k]
        following[r] = following[r] + 1

    first = jnp.int32(0)
    for r in range(row_tiles):
        used = following[r]
        following[r] = first
        first = first + ((used + 1) >> 1) * 2
    following[row_tiles] = jnp.int32(pairs.shape[0])

    @pl.loop(0, heads.shape[0], unroll=4)
    def _(i):
        heads[i] = row_tiles
        pairs[2 * i] = 128 * spans * row_tiles
        pairs[2 * i + 1] = 128 * spans * row_tiles

    swapped = odd[0] == 1

    @pl.loop(0, count, unroll=4)
    def _(k):
        r = rows[k]
        place = following[r]
        following[r] = place + 1
        span = jnp.int32(0)
        for s in range(1, spans):
            span = span + (cols[k] >= s * row_tiles).astype(jnp.int32)
        even = jnp.where(span >= 2, span - 2, span + 3)
        other = jnp.where(span <= 2, 2 - span, 7 - span)
        buf = jnp.where(swapped, other, even)
        flat = buf * row_tiles + cols[k] - span * row_tiles

        @pl.when(r < row_tiles)
        def _():
            pairs[place] = k + 128 * flat
            heads[place >> 1] = r

    helps, share, lanes = extra.shape
    mine = cot_v.shape[1] // helps
    high = bias[...].astype(jnp.bfloat16)
    rest = bias[...] - high.astype(jnp.float32)
    middle = rest.astype(jnp.bfloat16)
    low = (rest - middle.astype(jnp.float32)).astype(jnp.bfloat16)
    lane = lax.broadcasted_iota(jnp.int32, (share, lanes - mine), 1)
    bias_parts = jnp.where(lane == 0, high, jnp.where(lane == 1, middle, low))
    for copy in copies:
        copy.wait()
    for h in range(helps):
        extra[h, :, :mine] = cot_v[:, h * mine : (h + 1) * mine]
        extra[h, :, mine:] = bias_parts


def middle_kernel(parts, weight_t, out):
    helps, length, width = out.shape
    share = width // helps
    mine = length - 2 * share
    total = parts[0, :mine].astype(jnp.float32)
    for s in range(1, helps):
        total = total + parts[s, :mine].astype(jnp.float32)
    agg = total.astype(jnp.bfloat16)
    cotb = jnp.concatenate([parts[s, mine:] for s in range(helps)], axis=0)
    extra = cotb[:, mine:].astype(jnp.float32)
    bias = extra[:, 0:1] + extra[:, 1:2] + extra[:, 2:3]
    pre = lax.dot_general(weight_t[...], agg, NT, preferred_element_type=jnp.float32) + bias
    decay = jnp.exp(jnp.minimum(pre, 0.0))
    slope = jnp.where(pre > 0.0, 1.0, decay)
    grad = (cotb[:, :mine].astype(jnp.float32) * slope).astype(jnp.bfloat16)
    back = lax.dot_general(
        grad, weight_t[...], TN, preferred_element_type=jnp.float32
    ).astype(jnp.bfloat16)
    terms = lax.dot_general(grad, agg, NN, preferred_element_type=jnp.float32).astype(jnp.bfloat16)
    result = jnp.where(pre > 0.0, pre, decay - 1.0).astype(jnp.bfloat16)
    sums = jnp.sum(grad.astype(jnp.float32), axis=1, keepdims=True)
    high = sums.astype(jnp.bfloat16)
    low = (sums - high.astype(jnp.float32)).astype(jnp.bfloat16)
    lane = lax.broadcasted_iota(jnp.int32, (width, width - mine), 1)
    sums = jnp.where(lane == 0, high, low)
    for h in range(helps):
        own = slice(h * share, (h + 1) * share)
        out[h, :mine, :] = back
        out[h, mine : mine + share, :] = terms[own]
        out[h, mine + share :, :mine] = result[own]
        out[h, mine + share :, mine:] = sums[own]


def divide_kernel(parts, back, out, total, side, sums_v, sems):
    helps, _, width = parts.shape
    mine = back.shape[0] // helps
    share = total.shape[1]
    copies = []
    for s in range(helps):
        copies.append(pltpu.make_async_copy(parts.at[s, mine:], side.at[s], sems.at[s]))
        copies.append(
            pltpu.make_async_copy(
                parts.at[s, :mine], back.at[s * mine : (s + 1) * mine], sems.at[helps + s]
            )
        )
    for copy in copies:
        copy.start()
    for copy in copies[0::2]:
        copy.wait()
    sums = side[0].astype(jnp.float32)
    for s in range(1, helps):
        sums = sums + side[s].astype(jnp.float32)
    both = sums[share:, mine : mine + 1] + sums[share:, mine + 1 : mine + 2]
    both = jnp.broadcast_to(both, (share, total.shape[2] - width))
    sums_v[:, :width] = sums[:share]
    sums_v[:, width:] = both
    copies = copies[1::2]
    for s in range(total.shape[0]):
        copies.append(pltpu.make_async_copy(sums_v, total.at[s], sems.at[2 * helps + s]))
        copies[helps + s].start()
    for s in range(helps):
        out[:, s * mine : (s + 1) * mine] = side[s, share:, :mine]
    for copy in copies:
        copy.wait()


def spread(x):
    return lax.all_to_all(x, "help", 0, 0)


def alike(blks, steps):
    return [[b for b in range(blks) if b & ~steps == base] for base in range(blks) if base & steps == 0]


def per_device(features_t, weight, bias, cotangent_t, tile_vals, slot_row, slot_col):
    tiles = tile_vals[0, 0]
    tile = tiles.shape[-1]
    width, nodes = features_t.shape
    row_tiles = nodes // tile
    helps = lax.axis_size("help")
    blks = lax.axis_size("blk")
    share = cotangent_t.shape[0]
    mine = nodes // helps
    count = tiles.shape[0]
    swap = lambda b, h: (b ^ 1, h)

    zero, one, two = near(features_t)
    pair_count = (count + row_tiles + 3) // 4 * 2
    pairs, heads, extra, weight_t, tiles, own = pl.pallas_call(
        functools.partial(prepare_kernel, row_tiles),
        out_shape=(
            jax.ShapeDtypeStruct((2 * pair_count,), jnp.int32),
            jax.ShapeDtypeStruct((pair_count,), jnp.int32),
            jax.ShapeDtypeStruct((helps, share, width), jnp.bfloat16),
            jax.ShapeDtypeStruct(weight.shape, jnp.bfloat16),
            pltpu.VMEM(tiles.shape, jnp.bfloat16),
            pltpu.VMEM(features_t.shape, jnp.bfloat16),
        ),
        in_specs=[SMEM] * 3 + [VMEM] * 2 + [ANY] * 3,
        out_specs=(SMEM,) * 2 + (VMEM,) * 2 + (ANY,) * 2,
        scratch_shapes=[
            pltpu.SMEM((row_tiles + 1,), jnp.int32),
            pltpu.VMEM(cotangent_t.shape, jnp.bfloat16),
            pltpu.SemaphoreType.DMA((3,)),
        ],
        compiler_params=pltpu.CompilerParams(vmem_limit_bytes=4 * 2**20),
    )(
        (lax.axis_index("blk") % 2).astype(jnp.int32).reshape(1),
        slot_row[0, 0],
        slot_col[0, 0],
        bias.reshape(share, 1),
        weight,
        *(pltpu.with_memory_space_constraint(x, pltpu.HBM) for x in (tiles, cotangent_t, features_t)),
    )
    slots = (pairs, heads)
    three = move(after(one, own), swap)
    sent = aggregate(
        forward_kernel,
        (own, zero, one, two, three),
        tiles,
        slots,
        (helps, mine + share, width),
        extra,
    )
    length = mine + 2 * share
    sent = pl.pallas_call(
        middle_kernel,
        out_shape=jax.ShapeDtypeStruct((helps, length, width), jnp.bfloat16),
        in_specs=[VMEM] * 2,
        out_specs=VMEM,
        compiler_params=pltpu.CompilerParams(vmem_limit_bytes=16 * 2**20),
    )(spread(sent), weight_t)
    back, output, total = pl.pallas_call(
        divide_kernel,
        out_shape=(
            pltpu.VMEM((nodes, width), jnp.bfloat16),
            jax.ShapeDtypeStruct((share, nodes), jnp.bfloat16),
            pltpu.HBM((8, share, width + tile), jnp.float32),
        ),
        in_specs=[ANY],
        out_specs=(ANY, VMEM, ANY),
        scratch_shapes=[
            pltpu.VMEM((helps, 2 * share, width), jnp.bfloat16),
            pltpu.VMEM((share, width + tile), jnp.float32),
            pltpu.SemaphoreType.DMA((2 * helps + 8,)),
        ],
        compiler_params=pltpu.CompilerParams(vmem_limit_bytes=4 * 2**20),
    )(spread(sent))
    zero, one, two = near(back)
    half = blks // 2
    far = lax.all_to_all(total, "blk", 0, 0, axis_index_groups=alike(blks, half | 3))
    total = jnp.sum(far, axis=0)
    three = move(one, swap)
    value = aggregate(
        backward_kernel, (back, zero, one, two, three), tiles, slots, (helps, share, nodes)
    )
    propagated = jnp.sum(spread(value).astype(jnp.float32), axis=0)
    for step in (16, 8, 4):
        total = total + move(total, functools.partial(lambda s, b, h: (b ^ s, h), step))
    total = total * (1.0 / math.sqrt(nodes * blks))
    return (output, propagated, total[:, :width].T, total[:, width])


def solution(mesh):
    placed = (
        P(None, "blk"),
        P(),
        P("help"),
        P("help", "blk"),
        P("blk", "help", None, None, None),
        P("blk", "help", None),
        P("blk", "help", None),
    )
    return jax.shard_map(
        per_device,
        mesh=mesh,
        in_specs=placed,
        out_specs=(P("help", "blk"), P("help", "blk"), P(None, "help"), P("help")),
        check_vma=False,
    )
```

```python
import functools
import math

import jax
import jax.numpy as jnp
from jax import lax
from jax.experimental import pallas as pl
from jax.experimental.pallas import tpu as pltpu
from jax.sharding import PartitionSpec as P

BAND = 2
AXES = ("blk", "help")
ANY = pl.BlockSpec(memory_space=pl.ANY)
VMEM = pl.BlockSpec(memory_space=pltpu.VMEM)
SMEM = pl.BlockSpec(memory_space=pltpu.SMEM)
NT = (((1,), (1,)), ((), ()))
NN = (((1,), (0,)), ((), ()))
TN = (((0,), (0,)), ((), ()))


def move(block, source):
    blks, helps = lax.axis_size("blk"), lax.axis_size("help")
    route = []
    for b in range(blks):
        for h in range(helps):
            sb, sh = source(b, h)
            route.append(((sb % blks) * helps + sh, b * helps + h))
    return lax.ppermute(block, AXES, route)


def step_two(b, h, sign, blks):
    other = (b + 2 * sign) % blks
    half = blks // 2
    return (other, h if other // half == b // half else h ^ 1)


def after(value, other):
    return lax.optimization_barrier((value, other))[0]


def near(block):
    blks = lax.axis_size("blk")
    one = move(block, lambda b, h: step_two(b, h, 1 if b % 2 == 0 else -1, blks))
    zero = move(block, lambda b, h: (b ^ 1, h))
    two = move(block, lambda b, h: step_two(b, h, -1 if b % 2 == 0 else 1, blks))
    return zero, one, two


def unit(size):
    place = (size, size)
    return (
        lax.broadcasted_iota(jnp.int32, place, 0) == lax.broadcasted_iota(jnp.int32, place, 1)
    ).astype(jnp.bfloat16)


def load_all(refs, places, sems):
    copies = [
        pltpu.make_async_copy(ref, place, sems.at[i])
        for i, (ref, place) in enumerate(zip(refs, places))
    ]
    for copy in copies:
        copy.start()
    return copies


def add_pairs(pairs, rows, tiles, acc, piece, axis, dims):
    tile = tiles.shape[1]
    count = rows.shape[0]
    unroll = count // 2

    @pl.loop(0, count // unroll)
    def _(step):
        for j in range(unroll):
            i = step * unroll + j
            one, two = pairs[2 * i], pairs[2 * i + 1]
            left = jnp.concatenate([tiles[one & 127], tiles[two & 127]], axis=1)
            right = jnp.concatenate(
                [piece(pl.multiple_of((s >> 7) * tile, tile)) for s in (one, two)], axis=axis
            )
            product = lax.dot_general(left, right, dims, preferred_element_type=jnp.float32)
            acc[pl.ds(pl.multiple_of(rows[i] * tile, tile), tile), :] += product


def forward_kernel(pairs, rows, b0, b1, b2, b3, b4, tiles, extra, out, win, acc, sems, stage, out_sems):
    tile = tiles.shape[1]
    nodes = b0.shape[1]
    helps = out.shape[0]
    mine = nodes // helps
    refs = (b0, b1, b2, b3, b4)
    copies = load_all(refs, [win.at[:, i * nodes : (i + 1) * nodes] for i in range(5)], sems)
    leaving = []
    for h in range(helps):
        leaving.append(pltpu.make_async_copy(extra.at[h], out.at[h, mine:], out_sems.at[helps + h]))
        leaving[h].start()
    acc[...] = jnp.zeros_like(acc)
    win[:, 5 * nodes :] = jnp.zeros((win.shape[0], tile), jnp.bfloat16)
    for copy in copies:
        copy.wait()
    add_pairs(pairs, rows, tiles, acc, lambda c: win[:, pl.ds(c, tile)], 1, NT)
    for h in range(helps):
        stage[h] = acc[h * mine : (h + 1) * mine, :].astype(jnp.bfloat16)
        leaving.append(pltpu.make_async_copy(stage.at[h], out.at[h, :mine], out_sems.at[h]))
        leaving[helps + h].start()
    for copy in leaving:
        copy.wait()


def backward_kernel(pairs, rows, b0, b1, b2, b3, b4, tiles, out, win, acc, sems, stage, out_sems):
    tile = tiles.shape[1]
    helps, share, nodes = out.shape
    width = helps * share
    refs = (b0, b1, b2, b3, b4)
    copies = load_all(refs, [win.at[i * nodes : (i + 1) * nodes, :] for i in range(5)], sems)
    acc[...] = jnp.zeros_like(acc)
    win[5 * nodes :, :] = jnp.zeros((tile, win.shape[1]), jnp.bfloat16)
    for copy in copies:
        copy.wait()
    add_pairs(pairs, rows, tiles, acc, lambda c: win[pl.ds(c, tile), :], 0, NN)
    eye = unit(width)
    for t in range(nodes // tile):
        part = acc[t * tile : (t + 1) * tile, :].astype(jnp.bfloat16)
        turned = lax.dot_general(eye, part, NT, preferred_element_type=jnp.float32)
        stage[:, :, t * tile : (t + 1) * tile] = turned.astype(jnp.bfloat16).reshape(helps, share, tile)
    leaving = [pltpu.make_async_copy(stage.at[h], out.at[h], out_sems.at[h]) for h in range(helps)]
    for copy in leaving:
        copy.start()
    for copy in leaving:
        copy.wait()


def aggregate(kernel, blocks, tiles, slots, out_shape, *extra):
    count, tile = tiles.shape[0], tiles.shape[1]
    nodes = max(blocks[0].shape)
    width = min(blocks[0].shape)
    forward = blocks[0].shape[1] == nodes
    span = 5 * nodes + tile
    parts = out_shape[0]
    return pl.pallas_call(
        kernel,
        out_shape=pltpu.HBM(out_shape, jnp.bfloat16),
        in_specs=[SMEM] * 2 + [ANY] * 5 + [VMEM] + [ANY] * len(extra),
        out_specs=ANY,
        scratch_shapes=[
            pltpu.VMEM((width, span) if forward else (span, width), jnp.bfloat16),
            pltpu.VMEM((nodes + tile, width), jnp.float32),
            pltpu.SemaphoreType.DMA((5,)),
            pltpu.VMEM((parts, nodes // parts, width) if forward else out_shape, jnp.bfloat16),
            pltpu.SemaphoreType.DMA((2 * parts,)),
        ],
        compiler_params=pltpu.CompilerParams(vmem_limit_bytes=20 * 2**20),
        cost_estimate=pl.CostEstimate(
            flops=2 * count * tile * tile * width,
            bytes_accessed=6 * 2**20,
            transcendentals=0,
        ),
    )(*slots, *blocks, tiles, *extra)


def prepare_kernel(row_tiles, odd, rows, cols, bias, weight, tiles, cot, own, pairs, heads, extra, weight_t, tiles_v, own_v, following, cot_v, sems):
    copies = load_all((tiles, cot, own), (tiles_v, cot_v, own_v), sems)
    weight_t[...] = lax.dot_general(
        unit(weight.shape[0]), weight[...], NT, preferred_element_type=jnp.float32
    ).astype(jnp.bfloat16)
    spans = 2 * BAND + 1
    count = rows.shape[0]
    for r in range(row_tiles + 1):
        following[r] = 0

    @pl.loop(0, count, unroll=4)
    def _(k):
        r = rows[k]
        following[r] = following[r] + 1

    first = jnp.int32(0)
    for r in range(row_tiles):
        used = following[r]
        following[r] = first
        first = first + ((used + 1) >> 1) * 2
    following[row_tiles] = jnp.int32(pairs.shape[0])

    @pl.loop(0, heads.shape[0], unroll=4)
    def _(i):
        heads[i] = row_tiles
        pairs[2 * i] = 128 * spans * row_tiles
        pairs[2 * i + 1] = 128 * spans * row_tiles

    swapped = odd[0] == 1

    @pl.loop(0, count, unroll=4)
    def _(k):
        r = rows[k]
        place = following[r]
        following[r] = place + 1
        span = jnp.int32(0)
        for s in range(1, spans):
            span = span + (cols[k] >= s * row_tiles).astype(jnp.int32)
        even = jnp.where(span >= 2, span - 2, span + 3)
        other = jnp.where(span <= 2, 2 - span, 7 - span)
        buf = jnp.where(swapped, other, even)
        flat = buf * row_tiles + cols[k] - span * row_tiles

        @pl.when(r < row_tiles)
        def _():
            pairs[place] = k + 128 * flat
            heads[place >> 1] = r

    helps, share, lanes = extra.shape
    mine = cot_v.shape[1] // helps
    high = bias[...].astype(jnp.bfloat16)
    rest = bias[...] - high.astype(jnp.float32)
    middle = rest.astype(jnp.bfloat16)
    low = (rest - middle.astype(jnp.float32)).astype(jnp.bfloat16)
    lane = lax.broadcasted_iota(jnp.int32, (share, lanes - mine), 1)
    bias_parts = jnp.where(lane == 0, high, jnp.where(lane == 1, middle, low))
    for copy in copies:
        copy.wait()
    for h in range(helps):
        extra[h, :, :mine] = cot_v[:, h * mine : (h + 1) * mine]
        extra[h, :, mine:] = bias_parts


def middle_kernel(parts, weight_t, out):
    helps, length, width = out.shape
    share = width // helps
    mine = length - 2 * share
    total = parts[0, :mine].astype(jnp.float32)
    for s in range(1, helps):
        total = total + parts[s, :mine].astype(jnp.float32)
    agg = total.astype(jnp.bfloat16)
    cotb = jnp.concatenate([parts[s, mine:] for s in range(helps)], axis=0)
    extra = cotb[:, mine:].astype(jnp.float32)
    bias = extra[:, 0:1] + extra[:, 1:2] + extra[:, 2:3]
    pre = lax.dot_general(weight_t[...], agg, NT, preferred_element_type=jnp.float32) + bias
    decay = jnp.exp(jnp.minimum(pre, 0.0))
    slope = jnp.where(pre > 0.0, 1.0, decay)
    grad = (cotb[:, :mine].astype(jnp.float32) * slope).astype(jnp.bfloat16)
    back = lax.dot_general(
        grad, weight_t[...], TN, preferred_element_type=jnp.float32
    ).astype(jnp.bfloat16)
    terms = lax.dot_general(grad, agg, NN, preferred_element_type=jnp.float32).astype(jnp.bfloat16)
    result = jnp.where(pre > 0.0, pre, decay - 1.0).astype(jnp.bfloat16)
    sums = jnp.sum(grad.astype(jnp.float32), axis=1, keepdims=True)
    high = sums.astype(jnp.bfloat16)
    low = (sums - high.astype(jnp.float32)).astype(jnp.bfloat16)
    lane = lax.broadcasted_iota(jnp.int32, (width, width - mine), 1)
    sums = jnp.where(lane == 0, high, low)
    for h in range(helps):
        own = slice(h * share, (h + 1) * share)
        out[h, :mine, :] = back
        out[h, mine : mine + share, :] = terms[own]
        out[h, mine + share :, :mine] = result[own]
        out[h, mine + share :, mine:] = sums[own]


def divide_kernel(parts, back, out, total, side, sums_v, sems):
    helps, _, width = parts.shape
    mine = back.shape[0] // helps
    share = total.shape[1]
    copies = []
    for s in range(helps):
        copies.append(pltpu.make_async_copy(parts.at[s, mine:], side.at[s], sems.at[s]))
        copies.append(
            pltpu.make_async_copy(
                parts.at[s, :mine], back.at[s * mine : (s + 1) * mine], sems.at[helps + s]
            )
        )
    for copy in copies:
        copy.start()
    for copy in copies[0::2]:
        copy.wait()
    sums = side[0].astype(jnp.float32)
    for s in range(1, helps):
        sums = sums + side[s].astype(jnp.float32)
    both = sums[share:, mine : mine + 1] + sums[share:, mine + 1 : mine + 2]
    both = jnp.broadcast_to(both, (share, total.shape[2] - width))
    sums_v[:, :width] = sums[:share]
    sums_v[:, width:] = both
    copies = copies[1::2]
    for s in range(total.shape[0]):
        copies.append(pltpu.make_async_copy(sums_v, total.at[s], sems.at[2 * helps + s]))
        copies[helps + s].start()
    for s in range(helps):
        out[:, s * mine : (s + 1) * mine] = side[s, share:, :mine]
    for copy in copies:
        copy.wait()


def spread(x):
    return lax.all_to_all(x, "help", 0, 0)


def alike(blks, steps):
    return [[b for b in range(blks) if b & ~steps == base] for base in range(blks) if base & steps == 0]


def per_device(features_t, weight, bias, cotangent_t, tile_vals, slot_row, slot_col):
    tiles = tile_vals[0, 0]
    tile = tiles.shape[-1]
    width, nodes = features_t.shape
    row_tiles = nodes // tile
    helps = lax.axis_size("help")
    blks = lax.axis_size("blk")
    share = cotangent_t.shape[0]
    mine = nodes // helps
    count = tiles.shape[0]
    swap = lambda b, h: (b ^ 1, h)

    zero, one, two = near(features_t)
    pair_count = (count + row_tiles + 3) // 4 * 2
    pairs, heads, extra, weight_t, tiles, own = pl.pallas_call(
        functools.partial(prepare_kernel, row_tiles),
        out_shape=(
            jax.ShapeDtypeStruct((2 * pair_count,), jnp.int32),
            jax.ShapeDtypeStruct((pair_count,), jnp.int32),
            jax.ShapeDtypeStruct((helps, share, width), jnp.bfloat16),
            jax.ShapeDtypeStruct(weight.shape, jnp.bfloat16),
            pltpu.VMEM(tiles.shape, jnp.bfloat16),
            pltpu.VMEM(features_t.shape, jnp.bfloat16),
        ),
        in_specs=[SMEM] * 3 + [VMEM] * 2 + [ANY] * 3,
        out_specs=(SMEM,) * 2 + (VMEM,) * 2 + (ANY,) * 2,
        scratch_shapes=[
            pltpu.SMEM((row_tiles + 1,), jnp.int32),
            pltpu.VMEM(cotangent_t.shape, jnp.bfloat16),
            pltpu.SemaphoreType.DMA((3,)),
        ],
        compiler_params=pltpu.CompilerParams(vmem_limit_bytes=4 * 2**20),
    )(
        (lax.axis_index("blk") % 2).astype(jnp.int32).reshape(1),
        slot_row[0, 0],
        slot_col[0, 0],
        bias.reshape(share, 1),
        weight,
        *(pltpu.with_memory_space_constraint(x, pltpu.HBM) for x in (tiles, cotangent_t, features_t)),
    )
    slots = (pairs, heads)
    three = move(after(one, own), swap)
    sent = aggregate(
        forward_kernel,
        (own, zero, one, two, three),
        tiles,
        slots,
        (helps, mine + share, width),
        extra,
    )
    length = mine + 2 * share
    sent = pl.pallas_call(
        middle_kernel,
        out_shape=jax.ShapeDtypeStruct((helps, length, width), jnp.bfloat16),
        in_specs=[VMEM] * 2,
        out_specs=VMEM,
        compiler_params=pltpu.CompilerParams(vmem_limit_bytes=16 * 2**20),
    )(spread(sent), weight_t)
    back, output, total = pl.pallas_call(
        divide_kernel,
        out_shape=(
            pltpu.VMEM((nodes, width), jnp.bfloat16),
            jax.ShapeDtypeStruct((share, nodes), jnp.bfloat16),
            pltpu.HBM((8, share, width + tile), jnp.float32),
        ),
        in_specs=[ANY],
        out_specs=(ANY, VMEM, ANY),
        scratch_shapes=[
            pltpu.VMEM((helps, 2 * share, width), jnp.bfloat16),
            pltpu.VMEM((share, width + tile), jnp.float32),
            pltpu.SemaphoreType.DMA((2 * helps + 8,)),
        ],
        compiler_params=pltpu.CompilerParams(vmem_limit_bytes=4 * 2**20),
    )(spread(sent))
    zero, one, two = near(back)
    half = blks // 2
    far = lax.all_to_all(total, "blk", 0, 0, axis_index_groups=alike(blks, half | 3))
    total = jnp.sum(far, axis=0)
    three = move(one, swap)
    value = aggregate(
        backward_kernel, (back, zero, one, two, three), tiles, slots, (helps, share, nodes)
    )
    propagated = jnp.sum(spread(value).astype(jnp.float32), axis=0)
    flip = lambda s: functools.partial(lambda s, b, h: (b ^ s, h), s)
    total = (total + move(total, flip(4))) + (move(total, flip(8)) + move(total, flip(12)))
    total = total + move(total, flip(16))
    total = total * (1.0 / math.sqrt(nodes * blks))
    return (output, propagated, total[:, :width].T, total[:, width])


def solution(mesh):
    placed = (
        P(None, "blk"),
        P(),
        P("help"),
        P("help", "blk"),
        P("blk", "help", None, None, None),
        P("blk", "help", None),
        P("blk", "help", None),
    )
    return jax.shard_map(
        per_device,
        mesh=mesh,
        in_specs=placed,
        out_specs=(P("help", "blk"), P("help", "blk"), P(None, "help"), P("help")),
        check_vma=False,
    )
```

```python
import functools
import math

import jax
import jax.numpy as jnp
from jax import lax
from jax.experimental import pallas as pl
from jax.experimental.pallas import tpu as pltpu
from jax.sharding import PartitionSpec as P

BAND = 2
AXES = ("blk", "help")
ANY = pl.BlockSpec(memory_space=pl.ANY)
VMEM = pl.BlockSpec(memory_space=pltpu.VMEM)
SMEM = pl.BlockSpec(memory_space=pltpu.SMEM)
NT = (((1,), (1,)), ((), ()))
NN = (((1,), (0,)), ((), ()))
TN = (((0,), (0,)), ((), ()))


def move(block, source):
    blks, helps = lax.axis_size("blk"), lax.axis_size("help")
    route = []
    for b in range(blks):
        for h in range(helps):
            sb, sh = source(b, h)
            route.append(((sb % blks) * helps + sh, b * helps + h))
    return lax.ppermute(block, AXES, route)


def step_two(b, h, sign, blks):
    other = (b + 2 * sign) % blks
    half = blks // 2
    return (other, h if other // half == b // half else h ^ 1)


def after(value, other):
    return lax.optimization_barrier((value, other))[0]


def near(block):
    blks = lax.axis_size("blk")
    one = move(block, lambda b, h: step_two(b, h, 1 if b % 2 == 0 else -1, blks))
    zero = move(block, lambda b, h: (b ^ 1, h))
    two = move(block, lambda b, h: step_two(b, h, -1 if b % 2 == 0 else 1, blks))
    return zero, one, two


def unit(size):
    place = (size, size)
    return (
        lax.broadcasted_iota(jnp.int32, place, 0) == lax.broadcasted_iota(jnp.int32, place, 1)
    ).astype(jnp.bfloat16)


def load_all(refs, places, sems):
    copies = [
        pltpu.make_async_copy(ref, place, sems.at[i])
        for i, (ref, place) in enumerate(zip(refs, places))
    ]
    for copy in copies:
        copy.start()
    return copies


def add_pairs(pairs, rows, tiles, acc, piece, axis, dims):
    tile = tiles.shape[1]
    count = rows.shape[0]
    unroll = count // 2

    @pl.loop(0, count // unroll)
    def _(step):
        for j in range(unroll):
            i = step * unroll + j
            one, two = pairs[2 * i], pairs[2 * i + 1]
            left = jnp.concatenate([tiles[one & 127], tiles[two & 127]], axis=1)
            right = jnp.concatenate(
                [piece(pl.multiple_of((s >> 7) * tile, tile)) for s in (one, two)], axis=axis
            )
            product = lax.dot_general(left, right, dims, preferred_element_type=jnp.float32)
            acc[pl.ds(pl.multiple_of(rows[i] * tile, tile), tile), :] += product


def forward_kernel(pairs, rows, b0, b1, b2, b3, b4, tiles, extra, out, win, acc, sems, stage, out_sems):
    tile = tiles.shape[1]
    nodes = b0.shape[1]
    helps = out.shape[0]
    mine = nodes // helps
    refs = (b0, b1, b2, b3, b4)
    copies = load_all(refs, [win.at[:, i * nodes : (i + 1) * nodes] for i in range(5)], sems)
    leaving = []
    for h in range(helps):
        leaving.append(pltpu.make_async_copy(extra.at[h], out.at[h, mine:], out_sems.at[helps + h]))
        leaving[h].start()
    acc[...] = jnp.zeros_like(acc)
    win[:, 5 * nodes :] = jnp.zeros((win.shape[0], tile), jnp.bfloat16)
    for copy in copies:
        copy.wait()
    add_pairs(pairs, rows, tiles, acc, lambda c: win[:, pl.ds(c, tile)], 1, NT)
    for h in range(helps):
        stage[h] = acc[h * mine : (h + 1) * mine, :].astype(jnp.bfloat16)
        leaving.append(pltpu.make_async_copy(stage.at[h], out.at[h, :mine], out_sems.at[h]))
        leaving[helps + h].start()
    for copy in leaving:
        copy.wait()


def backward_kernel(pairs, rows, b0, b1, b2, b3, b4, tiles, out, win, acc, sems, stage, out_sems):
    tile = tiles.shape[1]
    helps, share, nodes = out.shape
    width = helps * share
    refs = (b0, b1, b2, b3, b4)
    copies = load_all(refs, [win.at[i * nodes : (i + 1) * nodes, :] for i in range(5)], sems)
    acc[...] = jnp.zeros_like(acc)
    win[5 * nodes :, :] = jnp.zeros((tile, win.shape[1]), jnp.bfloat16)
    for copy in copies:
        copy.wait()
    add_pairs(pairs, rows, tiles, acc, lambda c: win[pl.ds(c, tile), :], 0, NN)
    eye = unit(width)
    for t in range(nodes // tile):
        part = acc[t * tile : (t + 1) * tile, :].astype(jnp.bfloat16)
        turned = lax.dot_general(eye, part, NT, preferred_element_type=jnp.float32)
        stage[:, :, t * tile : (t + 1) * tile] = turned.astype(jnp.bfloat16).reshape(helps, share, tile)
    leaving = [pltpu.make_async_copy(stage.at[h], out.at[h], out_sems.at[h]) for h in range(helps)]
    for copy in leaving:
        copy.start()
    for copy in leaving:
        copy.wait()


def aggregate(kernel, blocks, tiles, slots, out_shape, *extra):
    count, tile = tiles.shape[0], tiles.shape[1]
    nodes = max(blocks[0].shape)
    width = min(blocks[0].shape)
    forward = blocks[0].shape[1] == nodes
    span = 5 * nodes + tile
    parts = out_shape[0]
    return pl.pallas_call(
        kernel,
        out_shape=pltpu.HBM(out_shape, jnp.bfloat16),
        in_specs=[SMEM] * 2 + [ANY] * 5 + [VMEM] + [ANY] * len(extra),
        out_specs=ANY,
        scratch_shapes=[
            pltpu.VMEM((width, span) if forward else (span, width), jnp.bfloat16),
            pltpu.VMEM((nodes + tile, width), jnp.float32),
            pltpu.SemaphoreType.DMA((5,)),
            pltpu.VMEM((parts, nodes // parts, width) if forward else out_shape, jnp.bfloat16),
            pltpu.SemaphoreType.DMA((2 * parts,)),
        ],
        compiler_params=pltpu.CompilerParams(vmem_limit_bytes=20 * 2**20),
        cost_estimate=pl.CostEstimate(
            flops=2 * count * tile * tile * width,
            bytes_accessed=6 * 2**20,
            transcendentals=0,
        ),
    )(*slots, *blocks, tiles, *extra)


def prepare_kernel(row_tiles, odd, rows, cols, bias, weight, tiles, cot, own, pairs, heads, extra, weight_t, tiles_v, own_v, following, cot_v, sems):
    copies = load_all((tiles, cot, own), (tiles_v, cot_v, own_v), sems)
    weight_t[...] = lax.dot_general(
        unit(weight.shape[0]), weight[...], NT, preferred_element_type=jnp.float32
    ).astype(jnp.bfloat16)
    spans = 2 * BAND + 1
    count = rows.shape[0]
    for r in range(row_tiles + 1):
        following[r] = 0

    @pl.loop(0, count, unroll=4)
    def _(k):
        r = rows[k]
        following[r] = following[r] + 1

    first = jnp.int32(0)
    for r in range(row_tiles):
        used = following[r]
        following[r] = first
        first = first + ((used + 1) >> 1) * 2
    following[row_tiles] = jnp.int32(pairs.shape[0])

    @pl.loop(0, heads.shape[0], unroll=4)
    def _(i):
        heads[i] = row_tiles
        pairs[2 * i] = 128 * spans * row_tiles
        pairs[2 * i + 1] = 128 * spans * row_tiles

    swapped = odd[0] == 1

    @pl.loop(0, count, unroll=4)
    def _(k):
        r = rows[k]
        place = following[r]
        following[r] = place + 1
        span = jnp.int32(0)
        for s in range(1, spans):
            span = span + (cols[k] >= s * row_tiles).astype(jnp.int32)
        even = jnp.where(span >= 2, span - 2, span + 3)
        other = jnp.where(span <= 2, 2 - span, 7 - span)
        buf = jnp.where(swapped, other, even)
        flat = buf * row_tiles + cols[k] - span * row_tiles

        @pl.when(r < row_tiles)
        def _():
            pairs[place] = k + 128 * flat
            heads[place >> 1] = r

    helps, share, lanes = extra.shape
    mine = cot_v.shape[1] // helps
    high = bias[...].astype(jnp.bfloat16)
    rest = bias[...] - high.astype(jnp.float32)
    middle = rest.astype(jnp.bfloat16)
    low = (rest - middle.astype(jnp.float32)).astype(jnp.bfloat16)
    lane = lax.broadcasted_iota(jnp.int32, (share, lanes - mine), 1)
    bias_parts = jnp.where(lane == 0, high, jnp.where(lane == 1, middle, low))
    for copy in copies:
        copy.wait()
    for h in range(helps):
        extra[h, :, :mine] = cot_v[:, h * mine : (h + 1) * mine]
        extra[h, :, mine:] = bias_parts


def middle_kernel(parts, weight_t, out):
    helps, length, width = out.shape
    share = width // helps
    mine = length - 2 * share
    total = parts[0, :mine].astype(jnp.float32)
    for s in range(1, helps):
        total = total + parts[s, :mine].astype(jnp.float32)
    agg = total.astype(jnp.bfloat16)
    cotb = jnp.concatenate([parts[s, mine:] for s in range(helps)], axis=0)
    extra = cotb[:, mine:].astype(jnp.float32)
    bias = extra[:, 0:1] + extra[:, 1:2] + extra[:, 2:3]
    pre = lax.dot_general(weight_t[...], agg, NT, preferred_element_type=jnp.float32) + bias
    decay = jnp.exp(jnp.minimum(pre, 0.0))
    slope = jnp.where(pre > 0.0, 1.0, decay)
    grad = (cotb[:, :mine].astype(jnp.float32) * slope).astype(jnp.bfloat16)
    back = lax.dot_general(
        grad, weight_t[...], TN, preferred_element_type=jnp.float32
    ).astype(jnp.bfloat16)
    terms = lax.dot_general(grad, agg, NN, preferred_element_type=jnp.float32).astype(jnp.bfloat16)
    result = jnp.where(pre > 0.0, pre, decay - 1.0).astype(jnp.bfloat16)
    sums = jnp.sum(grad.astype(jnp.float32), axis=1, keepdims=True)
    high = sums.astype(jnp.bfloat16)
    low = (sums - high.astype(jnp.float32)).astype(jnp.bfloat16)
    lane = lax.broadcasted_iota(jnp.int32, (width, width - mine), 1)
    sums = jnp.where(lane == 0, high, low)
    for h in range(helps):
        own = slice(h * share, (h + 1) * share)
        out[h, :mine, :] = back
        out[h, mine : mine + share, :] = terms[own]
        out[h, mine + share :, :mine] = result[own]
        out[h, mine + share :, mine:] = sums[own]


def divide_kernel(parts, back, out, total, side, sums_v, sems):
    helps, _, width = parts.shape
    mine = back.shape[0] // helps
    share = total.shape[1]
    copies = []
    for s in range(helps):
        copies.append(pltpu.make_async_copy(parts.at[s, mine:], side.at[s], sems.at[s]))
        copies.append(
            pltpu.make_async_copy(
                parts.at[s, :mine], back.at[s * mine : (s + 1) * mine], sems.at[helps + s]
            )
        )
    for copy in copies:
        copy.start()
    for copy in copies[0::2]:
        copy.wait()
    sums = side[0].astype(jnp.float32)
    for s in range(1, helps):
        sums = sums + side[s].astype(jnp.float32)
    both = sums[share:, mine : mine + 1] + sums[share:, mine + 1 : mine + 2]
    both = jnp.broadcast_to(both, (share, total.shape[2] - width))
    sums_v[:, :width] = sums[:share]
    sums_v[:, width:] = both
    copies = copies[1::2]
    for s in range(total.shape[0]):
        copies.append(pltpu.make_async_copy(sums_v, total.at[s], sems.at[2 * helps + s]))
        copies[helps + s].start()
    for s in range(helps):
        out[:, s * mine : (s + 1) * mine] = side[s, share:, :mine]
    for copy in copies:
        copy.wait()


def spread(x):
    return lax.all_to_all(x, "help", 0, 0)


def alike(blks, steps):
    return [[b for b in range(blks) if b & ~steps == base] for base in range(blks) if base & steps == 0]


def per_device(features_t, weight, bias, cotangent_t, tile_vals, slot_row, slot_col):
    tiles = tile_vals[0, 0]
    tile = tiles.shape[-1]
    width, nodes = features_t.shape
    row_tiles = nodes // tile
    helps = lax.axis_size("help")
    blks = lax.axis_size("blk")
    share = cotangent_t.shape[0]
    mine = nodes // helps
    count = tiles.shape[0]
    swap = lambda b, h: (b ^ 1, h)

    zero, one, two = near(features_t)
    pair_count = (count + row_tiles + 3) // 4 * 2
    pairs, heads, extra, weight_t, tiles, own = pl.pallas_call(
        functools.partial(prepare_kernel, row_tiles),
        out_shape=(
            jax.ShapeDtypeStruct((2 * pair_count,), jnp.int32),
            jax.ShapeDtypeStruct((pair_count,), jnp.int32),
            jax.ShapeDtypeStruct((helps, share, width), jnp.bfloat16),
            jax.ShapeDtypeStruct(weight.shape, jnp.bfloat16),
            pltpu.VMEM(tiles.shape, jnp.bfloat16),
            pltpu.VMEM(features_t.shape, jnp.bfloat16),
        ),
        in_specs=[SMEM] * 3 + [VMEM] * 2 + [ANY] * 3,
        out_specs=(SMEM,) * 2 + (VMEM,) * 2 + (ANY,) * 2,
        scratch_shapes=[
            pltpu.SMEM((row_tiles + 1,), jnp.int32),
            pltpu.VMEM(cotangent_t.shape, jnp.bfloat16),
            pltpu.SemaphoreType.DMA((3,)),
        ],
        compiler_params=pltpu.CompilerParams(vmem_limit_bytes=4 * 2**20),
    )(
        (lax.axis_index("blk") % 2).astype(jnp.int32).reshape(1),
        slot_row[0, 0],
        slot_col[0, 0],
        bias.reshape(share, 1),
        weight,
        *(pltpu.with_memory_space_constraint(x, pltpu.HBM) for x in (tiles, cotangent_t, features_t)),
    )
    slots = (pairs, heads)
    three = move(after(one, own), swap)
    sent = aggregate(
        forward_kernel,
        (own, zero, one, two, three),
        tiles,
        slots,
        (helps, mine + share, width),
        extra,
    )
    length = mine + 2 * share
    sent = pl.pallas_call(
        middle_kernel,
        out_shape=jax.ShapeDtypeStruct((helps, length, width), jnp.bfloat16),
        in_specs=[VMEM] * 2,
        out_specs=VMEM,
        compiler_params=pltpu.CompilerParams(vmem_limit_bytes=16 * 2**20),
    )(spread(sent), weight_t)
    back, output, total = pl.pallas_call(
        divide_kernel,
        out_shape=(
            pltpu.VMEM((nodes, width), jnp.bfloat16),
            jax.ShapeDtypeStruct((share, nodes), jnp.bfloat16),
            pltpu.HBM((8, share, width + tile), jnp.float32),
        ),
        in_specs=[ANY],
        out_specs=(ANY, VMEM, ANY),
        scratch_shapes=[
            pltpu.VMEM((helps, 2 * share, width), jnp.bfloat16),
            pltpu.VMEM((share, width + tile), jnp.float32),
            pltpu.SemaphoreType.DMA((2 * helps + 8,)),
        ],
        compiler_params=pltpu.CompilerParams(vmem_limit_bytes=4 * 2**20),
    )(spread(sent))
    zero, one, two = near(back)
    half = blks // 2
    far = lax.all_to_all(total, "blk", 0, 0, axis_index_groups=alike(blks, half | 3))
    total = jnp.sum(far, axis=0)
    three = move(one, swap)
    value = aggregate(
        backward_kernel, (back, zero, one, two, three), tiles, slots, (helps, share, nodes)
    )
    propagated = jnp.sum(spread(value).astype(jnp.float32), axis=0)
    flip = lambda s: functools.partial(lambda s, b, h: (b ^ s, h), s)
    total = after(total + move(total, flip(16)), value)
    total = (total + move(total, flip(4))) + (move(total, flip(8)) + move(total, flip(12)))
    total = total * (1.0 / math.sqrt(nodes * blks))
    return (output, propagated, total[:, :width].T, total[:, width])


def solution(mesh):
    placed = (
        P(None, "blk"),
        P(),
        P("help"),
        P("help", "blk"),
        P("blk", "help", None, None, None),
        P("blk", "help", None),
        P("blk", "help", None),
    )
    return jax.shard_map(
        per_device,
        mesh=mesh,
        in_specs=placed,
        out_specs=(P("help", "blk"), P("help", "blk"), P(None, "help"), P("help")),
        check_vma=False,
    )
```
